256 devices in a mesh: resp: 32 (over y_hi, z, core), head: 8 (over y_lo, x).
Axes of the slice: x: 4, y: 4 (y_hi: 2, y_lo: 2; y = y_hi * 2 + y_lo), z: 8, core: 2. Of those that a mesh axis runs over, the one named last changes fastest.
Arguments:
- upper_input: bfloat16 [2048, 5120], P('resp', 'head'), may hold values from -100 to 100
- upper_gain: bfloat16 [5120], P('head'), may hold values from 0.099609375 to 1.8984375
- upper_key_weight: bfloat16 [5120, 1024], P(None, 'head'), may hold values from -0.1875 to 0.1875
- upper_value_weight: bfloat16 [5120, 1024], P(None, 'head'), may hold values from -0.1875 to 0.1875
- upper_prompt_keys: bfloat16 [2048, 1024], P(None, 'head'), may hold values from -4.5 to 4.5
- upper_prompt_values: bfloat16 [2048, 1024], P(None, 'head'), may hold values from -6 to 6
- upper_queries: bfloat16 [4096, 8192], P('resp', 'head'), may hold values from -120 to 120
- upper_span_keys: bfloat16 [4096, 1024], P('resp', 'head'), may hold values from -16 to 16
- upper_span_values: bfloat16 [4096, 1024], P('resp', 'head'), may hold values from -6 to 6
- upper_out_grad: bfloat16 [4096, 8192], P('resp', 'head'), may hold values from -96 to 96
- lower_input: bfloat16 [2048, 5120], P('resp', 'head'), may hold values from -100 to 100
- lower_gain: bfloat16 [5120], P('head'), may hold values from 0.099609375 to 1.8984375
- lower_key_weight: bfloat16 [5120, 1024], P(None, 'head'), may hold values from -0.1875 to 0.1875
- lower_value_weight: bfloat16 [5120, 1024], P(None, 'head'), may hold values from -0.1875 to 0.1875
- lower_prompt_keys: bfloat16 [2048, 1024], P(None, 'head'), may hold values from -4.5 to 4.5
- lower_prompt_values: bfloat16 [2048, 1024], P(None, 'head'), may hold values from -6 to 6
- lower_queries: bfloat16 [4096, 8192], P('resp', 'head'), may hold values from -120 to 120
- lower_span_keys: bfloat16 [4096, 1024], P('resp', 'head'), may hold values from -16 to 16
- lower_span_values: bfloat16 [4096, 1024], P('resp', 'head'), may hold values from -6 to 6
- lower_out_grad: bfloat16 [4096, 8192], P('resp', 'head'), may hold values from -96 to 96
Outputs:
- upper_query_grads: bfloat16 [4096, 8192], P('resp', 'head')
- lower_query_grads: bfloat16 [4096, 8192], P('resp', 'head')
- upper_span_grads: bfloat16 [4096, 2048], P('resp', 'head')
- lower_span_grads: bfloat16 [4096, 2048], P('resp', 'head')
- prompt_grads: bfloat16 [2048, 5120], P('resp', 'head')
The draws below stay inside these ranges and needn't reach their ends.
All inputs are finite; a program needn't handle non-finite values.
Results may differ from the reference program's by a relative error of at most 0.02.
Values may be sent and summed in bfloat16 or wider, within the bound.
No kernel may reach another device: no remote copies, remote signals or barrier semaphores. Data moves between devices by JAX's collectives and lax.ppermute only.
A program may use at most 128 MiB of HBM per device.

```python
import math
import jax
import jax.numpy as jnp
from jax import lax

D = 5120
HD = 128
QPK = 8
KVH = 8
H = 64
C = 64
P_SIZE = 2048
RESPONSES = 64
TOKENS = 4096


def joint_keys(key, salt, blend):
    key = jax.random.fold_in(key, salt)
    first, second = jax.random.split(key, 2)
    keys = jnp.clip(jax.random.normal(first, (P_SIZE, KVH * HD), jnp.float32), -4.0, 4.0)
    queries = jnp.clip(jax.random.normal(second, (TOKENS, H * HD), jnp.float32), -4.0, 4.0)
    quarter = P_SIZE // 4
    rows = jnp.arange(P_SIZE)[:, None]
    band = ((rows >= quarter) & (rows < 2 * quarter)).astype(jnp.float32) * blend
    keys = keys * (1.0 - band)
    tokens = jnp.arange(TOKENS)
    chosen = (tokens % 16 == 3).astype(jnp.float32)[:, None] * blend
    queries = queries * (1.0 - chosen)
    return (keys, queries)


def prompt_rows(key):
    first = jax.random.fold_in(key, 0)
    third = jax.random.fold_in(key, 2)
    fourth = jax.random.fold_in(key, 3)
    base = jnp.clip(jax.random.normal(first, (P_SIZE, D), jnp.float32), -4.0, 4.0)
    row_scale = jnp.exp(jax.random.uniform(third, (P_SIZE, 1), jnp.float32, math.log(0.3), math.log(3.0)))
    ramp = 3.0 ** (jnp.arange(D, dtype=jnp.float32) / D)
    column = 0.6 * ramp[None, :] * jnp.exp(jax.random.uniform(fourth, (1, D), jnp.float32, -1.15, 1.15))
    values = base * row_scale * column
    return values.astype(jnp.bfloat16)


def draw_upper_prompt_keys(key, part):
    blend = 0.0
    return joint_keys(key, 11, blend)[0].astype(jnp.bfloat16)


def draw_upper_queries(key, part):
    blend = 0.0
    return joint_keys(key, 11, blend)[1].astype(jnp.bfloat16)


def draw_lower_prompt_keys(key, part):
    blend = 0.0
    return joint_keys(key, 12, blend)[0].astype(jnp.bfloat16)


def draw_lower_queries(key, part):
    blend = 0.0
    return joint_keys(key, 12, blend)[1].astype(jnp.bfloat16)


def draw_upper_input(key, part):
    key = jax.random.fold_in(key, 21)
    return prompt_rows(key)


def draw_lower_input(key, part):
    key = jax.random.fold_in(key, 22)
    return prompt_rows(key)


def steps_of(own_key, dims, cuts, smallest, largest):
    def one(dim, parts):
        draws = jax.random.uniform(jax.random.fold_in(jax.random.fold_in(own_key, 6), dim), (parts,), jnp.float32, smallest / len(cuts), largest / len(cuts))
        return jnp.repeat(jnp.exp(draws), dims[dim] // parts).reshape((-1,) + (1,) * (len(dims) - dim - 1))

    level = one(*cuts[0])
    for cut in cuts[1:]:
        level = level * one(*cut)
    return level


def bell_draw(stream_key, extent, width, reach, cuts=(), kind=jnp.bfloat16):
    loudness = steps_of(stream_key, extent, cuts, -0.22, 0.18) if cuts else 1.0
    array = jax.random.normal(stream_key, extent, jnp.float32) * width * loudness
    return jnp.minimum(jnp.maximum(array, -reach), reach).astype(kind)


def setup_inputs(seed: int = 0) -> dict:
    splits = jax.random.split(jax.random.key(seed), 21)
    upper_input = draw_upper_input(jax.random.fold_in(splits[20], 71), 0)
    upper_gain = jnp.clip(1.0 + 0.18 * jax.random.normal(splits[1], (D,), jnp.float32), 0.099609375, 1.8984375).astype(jnp.bfloat16)
    upper_key_weight = bell_draw(splits[2], (D, KVH * HD), (KVH * HD) ** -0.5, 0.1875, ((1, 8),))
    upper_value_weight = bell_draw(splits[3], (D, KVH * HD), (KVH * HD) ** -0.5, 0.1875, ((1, 8),))
    upper_prompt_keys = draw_upper_prompt_keys(jax.random.fold_in(splits[20], 71), 0)
    upper_prompt_values = bell_draw(splits[5], (P_SIZE, KVH * HD), 1.0, 6.0, ((1, 8),))
    upper_queries = draw_upper_queries(jax.random.fold_in(splits[20], 71), 0)
    upper_span_keys = bell_draw(splits[7], (TOKENS, KVH * HD), 2.5, 16.0, ((0, 32), (1, 8)))
    upper_span_values = bell_draw(splits[8], (TOKENS, KVH * HD), 1.0, 6.0, ((0, 32), (1, 8)))
    upper_out_grad = bell_draw(splits[9], (TOKENS, H * HD), 16.0, 96.0, ((0, 32), (1, 8)))
    lower_input = draw_lower_input(jax.random.fold_in(splits[20], 71), 0)
    lower_gain = jnp.clip(1.0 + 0.18 * jax.random.normal(splits[11], (D,), jnp.float32), 0.099609375, 1.8984375).astype(jnp.bfloat16)
    lower_key_weight = bell_draw(splits[12], (D, KVH * HD), (KVH * HD) ** -0.5, 0.1875, ((1, 8),))
    lower_value_weight = bell_draw(splits[13], (D, KVH * HD), (KVH * HD) ** -0.5, 0.1875, ((1, 8),))
    lower_prompt_keys = draw_lower_prompt_keys(jax.random.fold_in(splits[20], 71), 0)
    lower_prompt_values = bell_draw(splits[15], (P_SIZE, KVH * HD), 1.0, 6.0, ((1, 8),))
    lower_queries = draw_lower_queries(jax.random.fold_in(splits[20], 71), 0)
    lower_span_keys = bell_draw(splits[17], (TOKENS, KVH * HD), 2.5, 16.0, ((0, 32), (1, 8)))
    lower_span_values = bell_draw(splits[18], (TOKENS, KVH * HD), 1.0, 6.0, ((0, 32), (1, 8)))
    lower_out_grad = bell_draw(splits[19], (TOKENS, H * HD), 16.0, 96.0, ((0, 32), (1, 8)))
    return dict(upper_input=upper_input, upper_gain=upper_gain, upper_key_weight=upper_key_weight, upper_value_weight=upper_value_weight, upper_prompt_keys=upper_prompt_keys, upper_prompt_values=upper_prompt_values, upper_queries=upper_queries, upper_span_keys=upper_span_keys, upper_span_values=upper_span_values, upper_out_grad=upper_out_grad, lower_input=lower_input, lower_gain=lower_gain, lower_key_weight=lower_key_weight, lower_value_weight=lower_value_weight, lower_prompt_keys=lower_prompt_keys, lower_prompt_values=lower_prompt_values, lower_queries=lower_queries, lower_span_keys=lower_span_keys, lower_span_values=lower_span_values, lower_out_grad=lower_out_grad)


epsilon = 1e-06
masked = -1e+30

def rounded(values):
    return lax.optimization_barrier(values.astype(jnp.bfloat16)).astype(jnp.float32)

def head_grads(query, output_grad, keys, values, span_keys, span_values):
    scale = HD ** (-0.5)
    query = query.astype(jnp.float32)
    output_grad = output_grad.astype(jnp.float32)
    keys = keys.astype(jnp.float32)
    values = values.astype(jnp.float32)
    span_keys = span_keys.astype(jnp.float32)
    span_values = span_values.astype(jnp.float32)
    prompt_scores = jnp.einsum('rcd,jd->rcj', query, keys) * scale
    span_scores = jnp.einsum('rcd,rsd->rcs', query, span_keys) * scale
    causal = jnp.arange(C)[:, None] >= jnp.arange(C)[None, :]
    span_scores = jnp.where(causal[None], span_scores, masked)
    highest = jnp.maximum(lax.optimization_barrier(jnp.max(prompt_scores, axis=-1, keepdims=True)), lax.optimization_barrier(jnp.max(span_scores, axis=-1, keepdims=True)))
    prompt_exp = jnp.exp(prompt_scores - highest)
    span_exp = jnp.exp(span_scores - highest)
    total = lax.optimization_barrier(jnp.sum(prompt_exp, axis=-1, keepdims=True)) + lax.optimization_barrier(jnp.sum(span_exp, axis=-1, keepdims=True))
    prompt_weights = prompt_exp / total
    span_weights = span_exp / total
    prompt_dots = jnp.einsum('rcd,jd->rcj', output_grad, values)
    span_dots = jnp.einsum('rcd,rsd->rcs', output_grad, span_values)
    delta = lax.optimization_barrier(jnp.sum(prompt_weights * prompt_dots, axis=-1, keepdims=True)) + lax.optimization_barrier(jnp.sum(span_weights * span_dots, axis=-1, keepdims=True))
    prompt_slopes = rounded(prompt_weights * (prompt_dots - delta))
    span_slopes = rounded(span_weights * (span_dots - delta))
    prompt_rounded = rounded(prompt_weights)
    span_rounded = rounded(span_weights)
    query_grad = (jnp.einsum('rcj,jd->rcd', prompt_slopes, keys) + jnp.einsum('rcs,rsd->rcd', span_slopes, span_keys)) * scale
    key_grad = jnp.einsum('rcj,rcd->jd', prompt_slopes, query) * scale
    value_grad = jnp.einsum('rcj,rcd->jd', prompt_rounded, output_grad)
    span_key_grad = jnp.einsum('rcs,rcd->rsd', span_slopes, query) * scale
    span_value_grad = jnp.einsum('rcs,rcd->rsd', span_rounded, output_grad)
    return (query_grad, key_grad, value_grad, span_key_grad, span_value_grad)

def layer_grads(hidden_in, norm_gain, key_weight, value_weight, prompt_keys, prompt_values, queries, span_keys, span_values, out_grad):
    query_heads = queries.reshape(RESPONSES, C, KVH, QPK, HD).transpose(2, 3, 0, 1, 4)
    grad_heads = out_grad.reshape(RESPONSES, C, KVH, QPK, HD).transpose(2, 3, 0, 1, 4)
    key_heads = prompt_keys.reshape(P_SIZE, KVH, HD).transpose(1, 0, 2)
    value_heads = prompt_values.reshape(P_SIZE, KVH, HD).transpose(1, 0, 2)
    span_key_heads = span_keys.reshape(RESPONSES, C, KVH, HD).transpose(2, 0, 1, 3)
    span_value_heads = span_values.reshape(RESPONSES, C, KVH, HD).transpose(2, 0, 1, 3)

    def per_group(items):
        group_queries, group_grads, group_keys, group_values, group_ckeys, group_cvalues = items

        def per_head(pair):
            return head_grads(pair[0], pair[1], group_keys, group_values, group_ckeys, group_cvalues)
        results = lax.map(per_head, (group_queries, group_grads))
        return (results[0], lax.optimization_barrier(jnp.sum(results[1], axis=0)), lax.optimization_barrier(jnp.sum(results[2], axis=0)), lax.optimization_barrier(jnp.sum(results[3], axis=0)), lax.optimization_barrier(jnp.sum(results[4], axis=0)))
    query_grad, key_sum, value_sum, ckey_sum, cvalue_sum = lax.map(per_group, (query_heads, grad_heads, key_heads, value_heads, span_key_heads, span_value_heads))
    query_grad = query_grad.transpose(2, 3, 0, 1, 4).reshape(TOKENS, H * HD).astype(jnp.bfloat16)
    span_grad = jnp.stack([ckey_sum, cvalue_sum], axis=1).transpose(2, 3, 0, 1, 4)
    span_grad = span_grad.reshape(TOKENS, KVH * 2 * HD).astype(jnp.bfloat16)
    key_rows = key_sum.transpose(1, 0, 2).reshape(P_SIZE, KVH * HD).astype(jnp.bfloat16)
    value_rows = value_sum.transpose(1, 0, 2).reshape(P_SIZE, KVH * HD).astype(jnp.bfloat16)
    projected = jnp.dot(key_rows, key_weight.T, preferred_element_type=jnp.float32)
    projected = projected + jnp.dot(value_rows, value_weight.T, preferred_element_type=jnp.float32)
    hidden = hidden_in.astype(jnp.float32)
    inverse = lax.rsqrt(lax.optimization_barrier(jnp.mean(hidden * hidden, axis=1, keepdims=True)) + epsilon)
    scaled = norm_gain.astype(jnp.float32)[None, :] * projected
    hidden_grad = inverse * scaled - hidden * inverse ** 3 * lax.optimization_barrier(jnp.sum(scaled * hidden, axis=1, keepdims=True)) / D
    return (query_grad, span_grad, hidden_grad)

def reference(upper_input, upper_gain, upper_key_weight, upper_value_weight, upper_prompt_keys, upper_prompt_values, upper_queries, upper_span_keys, upper_span_values, upper_out_grad, lower_input, lower_gain, lower_key_weight, lower_value_weight, lower_prompt_keys, lower_prompt_values, lower_queries, lower_span_keys, lower_span_values, lower_out_grad):
    upper_query, upper_span, upper_hidden = layer_grads(upper_input, upper_gain, upper_key_weight, upper_value_weight, upper_prompt_keys, upper_prompt_values, upper_queries, upper_span_keys, upper_span_values, upper_out_grad)
    lower_query, lower_span, lower_hidden = layer_grads(lower_input, lower_gain, lower_key_weight, lower_value_weight, lower_prompt_keys, lower_prompt_values, lower_queries, lower_span_keys, lower_span_values, lower_out_grad)
    prompt_grads = (upper_hidden + lower_hidden).astype(jnp.bfloat16)
    return (upper_query, lower_query, upper_span, lower_span, prompt_grads)
```

```python
import jax
import jax.numpy as jnp
from jax import lax
from jax.experimental import pallas as pl
from jax.experimental.pallas import tpu as pltpu

HEAD = 128
C = 64
NT = (((1,), (1,)), ((), ()))


def attend_kernel(q_ref, g_ref, k_ref, v_ref, sk_ref, sv_ref, dq_ref, span_ref, kv_ref,
                  keys, values, keys_t, scores, dots, slopes, weights, queries, grads):
    step = pl.program_id(0)
    steps = pl.num_programs(0)
    tokens = q_ref.shape[0]
    pair = 2 * tokens
    prompt = k_ref.shape[0]
    rows = prompt + tokens
    scale = HEAD ** -0.5
    factor = scale * 1.4426950408889634
    chunk = 128
    count = rows // chunk

    @pl.when(step == 0)
    def _():
        keys[:prompt, :] = k_ref[...]
        keys[prompt:, :] = sk_ref[...]
        values[:prompt, :] = v_ref[...]
        values[prompt:, :] = sv_ref[...]
        for j in range(count):
            keys_t[:, j * chunk:(j + 1) * chunk] = keys[j * chunk:(j + 1) * chunk, :].T

    query = jnp.concatenate([q_ref[:, :HEAD], q_ref[:, HEAD:]], axis=0)
    grad = jnp.concatenate([g_ref[:, :HEAD], g_ref[:, HEAD:]], axis=0)
    place = pl.ds(pl.multiple_of(step * pair, pair), pair)
    queries[place, :] = query
    grads[place, :] = grad

    highest = jnp.full((8, pair), -1e30, jnp.float32)
    for j in range(count):
        part = slice(j * chunk, (j + 1) * chunk)
        block = lax.dot_general(keys[part, :], query, NT, preferred_element_type=jnp.float32)
        if j == count - 1:
            u = lax.broadcasted_iota(jnp.int32, block.shape, 0)
            t = lax.rem(lax.broadcasted_iota(jnp.int32, block.shape, 1), tokens)
            block = jnp.where((lax.div(u, C) == lax.div(t, C)) & (u <= t), block, -1e30)
        scores[part, :] = block
        highest = jnp.maximum(highest, jnp.max(block.reshape(chunk // 8, 8, pair), axis=0))
    highest = jnp.max(highest, axis=0, keepdims=True)

    total = jnp.zeros((8, pair), jnp.float32)
    delta = jnp.zeros((8, pair), jnp.float32)
    for j in range(count):
        part = slice(j * chunk, (j + 1) * chunk)
        block = jnp.exp2((scores[part, :] - highest) * factor)
        scores[part, :] = block
        dot = lax.dot_general(values[part, :], grad, NT, preferred_element_type=jnp.float32)
        dots[part, :] = dot
        total = total + jnp.sum(block.reshape(chunk // 8, 8, pair), axis=0)
        delta = delta + jnp.sum((block * dot).reshape(chunk // 8, 8, pair), axis=0)
    inverse = 1.0 / jnp.sum(total, axis=0, keepdims=True)
    delta = jnp.sum(delta, axis=0, keepdims=True) * inverse

    query_grad = jnp.zeros((HEAD, pair), jnp.float32)
    for j in range(count):
        part = slice(j * chunk, (j + 1) * chunk)
        weight = scores[part, :] * inverse
        slope = (weight * (dots[part, :] - delta)).astype(jnp.bfloat16)
        weights[part, place] = weight.astype(jnp.bfloat16)
        slopes[part, place] = slope
    query_grad = jnp.dot(keys_t[...], slopes[:, place], preferred_element_type=jnp.float32)
    query_grad = query_grad * scale
    dq_ref[:, :HEAD] = query_grad[:, :tokens].T.astype(jnp.bfloat16)
    dq_ref[:, HEAD:] = query_grad[:, tokens:].T.astype(jnp.bfloat16)

    @pl.when(step == steps - 1)
    def _():
        for j in range(count):
            part = slice(j * chunk, (j + 1) * chunk)
            key_part = jnp.dot(slopes[part, :], queries[...], preferred_element_type=jnp.float32)
            value_part = jnp.dot(weights[part, :], grads[...], preferred_element_type=jnp.float32)
            both = jnp.concatenate([key_part * scale, value_part], axis=1).astype(jnp.bfloat16)
            if j < count - 1:
                kv_ref[part, :] = both
            else:
                span_ref[...] = both


def attend(q, k, v, sk, sv, g):
    tokens = q.shape[0]
    heads = q.shape[1] // HEAD
    prompt = k.shape[0]
    rows = prompt + tokens
    pair = 2 * tokens
    whole = lambda shape: pl.BlockSpec(shape, lambda i: (0, 0))
    paired = pl.BlockSpec((tokens, 2 * HEAD), lambda i: (0, i))
    return pl.pallas_call(
        attend_kernel,
        grid=(heads // 2,),
        in_specs=[paired, paired, whole((prompt, HEAD)), whole((prompt, HEAD)),
                  whole((tokens, HEAD)), whole((tokens, HEAD))],
        out_specs=[paired, whole((tokens, 2 * HEAD)), whole((prompt, 2 * HEAD))],
        out_shape=[
            jax.ShapeDtypeStruct(q.shape, jnp.bfloat16),
            jax.ShapeDtypeStruct((tokens, 2 * HEAD), jnp.bfloat16),
            jax.ShapeDtypeStruct((prompt, 2 * HEAD), jnp.bfloat16),
        ],
        scratch_shapes=[
            pltpu.VMEM((rows, HEAD), jnp.bfloat16),
            pltpu.VMEM((rows, HEAD), jnp.bfloat16),
            pltpu.VMEM((HEAD, rows), jnp.bfloat16),
            pltpu.VMEM((rows, pair), jnp.float32),
            pltpu.VMEM((rows, pair), jnp.float32),
            pltpu.VMEM((rows, heads * tokens), jnp.bfloat16),
            pltpu.VMEM((rows, heads * tokens), jnp.bfloat16),
            pltpu.VMEM((heads * tokens, HEAD), jnp.bfloat16),
            pltpu.VMEM((heads * tokens, HEAD), jnp.bfloat16),
        ],
        compiler_params=pltpu.CompilerParams(vmem_limit_bytes=48 * 1024 * 1024),
        cost_estimate=pl.CostEstimate(flops=10 * rows * heads * tokens * HEAD, bytes_accessed=4 * 2**20, transcendentals=rows * heads * tokens),
    )(q, g, k, v, sk, sv)


from jax.sharding import PartitionSpec as P

D = 5120
epsilon = 1e-06
RESP = 32
CORE_SWAP = [(i, i ^ 1) for i in range(RESP)]
SAME_CORE = [[2 * i + c for i in range(RESP // 2)] for c in range(2)]


def reduce_resp(upper_kv, lower_kv):
    core = lax.rem(lax.axis_index("resp"), 2)
    parts = []
    for kv in (upper_kv, lower_kv):
        blocks = kv.reshape(RESP // 2, 2, -1, kv.shape[1])
        mine = lax.dynamic_index_in_dim(blocks, core, 1, keepdims=False)
        other = lax.dynamic_index_in_dim(blocks, 1 - core, 1, keepdims=False)
        got = lax.ppermute(other, "resp", CORE_SWAP)
        total = mine.astype(jnp.float32) + got.astype(jnp.float32)
        parts.append(total.astype(jnp.bfloat16))
    sent = jnp.stack(parts, axis=1)
    blocks = lax.all_to_all(sent, "resp", 0, 0, axis_index_groups=SAME_CORE)
    return jnp.sum(blocks.astype(jnp.float32), axis=0)


def head_part(rows, key_weight, value_weight, hidden, gain):
    rounded = rows.astype(jnp.bfloat16)
    projected = lax.dot_general(
        rounded[:, :HEAD], key_weight, NT, preferred_element_type=jnp.float32
    ) + lax.dot_general(rounded[:, HEAD:], value_weight, NT, preferred_element_type=jnp.float32)
    hidden = hidden.astype(jnp.float32)
    inverse = lax.rsqrt(jnp.mean(hidden * hidden, axis=1, keepdims=True) + epsilon)
    scaled = gain.astype(jnp.float32) * projected
    row_sums = jnp.sum(scaled * hidden, axis=1, keepdims=True)
    return inverse * scaled - hidden * (inverse**3 * row_sums / D)


def body(
    upper_input, upper_gain, upper_key_weight, upper_value_weight, upper_prompt_keys,
    upper_prompt_values, upper_queries, upper_span_keys, upper_span_values, upper_out_grad,
    lower_input, lower_gain, lower_key_weight, lower_value_weight, lower_prompt_keys,
    lower_prompt_values, lower_queries, lower_span_keys, lower_span_values, lower_out_grad,
):
    rows = upper_input.shape[0]
    width = upper_input.shape[1]
    packed = jnp.concatenate(
        [upper_input, lower_input, upper_gain[None], lower_gain[None]], axis=0
    )
    whole = lax.all_gather(packed, "head", axis=1, tiled=True)
    upper_query, upper_span, upper_kv = attend(
        upper_queries, upper_prompt_keys, upper_prompt_values, upper_span_keys,
        upper_span_values, upper_out_grad,
    )
    lower_query, lower_span, lower_kv = attend(
        lower_queries, lower_prompt_keys, lower_prompt_values, lower_span_keys,
        lower_span_values, lower_out_grad,
    )
    summed = reduce_resp(upper_kv, lower_kv)
    part = head_part(
        summed[0], upper_key_weight, upper_value_weight, whole[:rows], whole[2 * rows : 2 * rows + 1]
    ) + head_part(
        summed[1], lower_key_weight, lower_value_weight, whole[rows : 2 * rows], whole[2 * rows + 1 :]
    )
    blocks = part.astype(jnp.bfloat16).reshape(rows, -1, width).transpose(1, 0, 2)
    blocks = lax.all_to_all(blocks, "head", 0, 0)
    prompt_grads = jnp.sum(blocks.astype(jnp.float32), axis=0).astype(jnp.bfloat16)
    return (upper_query, lower_query, upper_span, lower_span, prompt_grads)


def solution(mesh):
    layer = (
        P("resp", "head"), P("head"), P(None, "head"), P(None, "head"), P(None, "head"),
        P(None, "head"), P("resp", "head"), P("resp", "head"), P("resp", "head"), P("resp", "head"),
    )
    return jax.shard_map(
        body,
        mesh=mesh,
        in_specs=layer + layer,
        out_specs=(P("resp", "head"),) * 5,
        check_vma=False,
    )
```

```python
import functools
import jax
import jax.numpy as jnp
from jax import lax
from jax.experimental import pallas as pl
from jax.experimental.pallas import tpu as pltpu
from jax.sharding import PartitionSpec as P

HEAD = 128
C = 64
NT = (((1,), (1,)), ((), ()))
TN = (((0,), (0,)), ((), ()))


def attend_kernel(core_ref, q_ref, g_ref, k_ref, v_ref, sk_ref, sv_ref, dq_ref, span_ref,
                  mine_ref, other_ref, scores, dots, key_sums, value_sums):
    tokens = q_ref.shape[0]
    prompt = k_ref.shape[0]
    group = 2
    pair = group * tokens
    pairs = q_ref.shape[1] // (group * HEAD)
    scale = HEAD ** -0.5
    factor = scale * 1.4426950408889634
    chunk = 2 * C
    count = prompt // chunk + 1
    parts = [slice(j * chunk, (j + 1) * chunk) for j in range(count)]
    even = core_ref[0] == 0

    def rows_of(ref, span, j):
        return ref[parts[j], :] if j < count - 1 else span[...]

    def stacked(ref, p):
        heads = [ref[:, h * HEAD:(h + 1) * HEAD] for h in range(group * p, group * p + group)]
        return jnp.concatenate(heads, axis=0)

    def first_pass(p, state):
        query = stacked(q_ref, p)
        grad = stacked(g_ref, p)
        tops = []
        totals = []
        deltas = []
        for j in range(count):
            block = lax.dot_general(
                rows_of(k_ref, sk_ref, j), query, NT, preferred_element_type=jnp.float32
            )
            if j == count - 1:
                u = lax.broadcasted_iota(jnp.int32, block.shape, 0)
                t = lax.rem(lax.broadcasted_iota(jnp.int32, block.shape, 1), tokens)
                block = jnp.where((lax.div(u, C) == lax.div(t, C)) & (u <= t), block, -1e30)
            top = jnp.max(block, axis=0, keepdims=True)
            block = jnp.exp2((block - top) * factor)
            scores[p, parts[j], :] = block
            dot = lax.dot_general(
                rows_of(v_ref, sv_ref, j), grad, NT, preferred_element_type=jnp.float32
            )
            dots[p, parts[j], :] = dot
            tops.append(top)
            totals.append(jnp.sum(block, axis=0, keepdims=True))
            deltas.append(jnp.sum(block * dot, axis=0, keepdims=True))
            yield
        tops = jnp.concatenate(tops, axis=0)
        weigh = jnp.exp2((tops - jnp.max(tops, axis=0, keepdims=True)) * factor)
        total = jnp.sum(weigh * jnp.concatenate(totals, axis=0), axis=0, keepdims=True)
        weigh = weigh / total
        delta = jnp.sum(weigh * jnp.concatenate(deltas, axis=0), axis=0, keepdims=True)
        state[p] = (query, grad, weigh, delta)

    def second_pass(p, state):
        query, grad, weigh, delta = state.pop(p)
        query_grad = jnp.zeros((pair, HEAD), jnp.float32)
        for j in range(count):
            weight = scores[p, parts[j], :] * weigh[j:j + 1, :]
            slope = (weight * (dots[p, parts[j], :] - delta)).astype(jnp.bfloat16)
            weight = weight.astype(jnp.bfloat16)
            query_grad = query_grad + lax.dot_general(
                slope, rows_of(k_ref, sk_ref, j), TN, preferred_element_type=jnp.float32
            )
            key_sum = jnp.dot(slope, query, preferred_element_type=jnp.float32)
            value_sum = jnp.dot(weight, grad, preferred_element_type=jnp.float32)
            if p > 0:
                key_sum = key_sum + key_sums[parts[j], :]
                value_sum = value_sum + value_sums[parts[j], :]
            if p < pairs - 1:
                key_sums[parts[j], :] = key_sum
                value_sums[parts[j], :] = value_sum
            else:
                both = jnp.concatenate([key_sum * scale, value_sum], axis=1)
                if j == count - 1:
                    span_ref[...] = both.astype(jnp.bfloat16)
                else:
                    half = slice(j * C, (j + 1) * C)
                    mine_ref[half, :] = jnp.where(even, both[:C], both[C:]).astype(jnp.bfloat16)
                    other_ref[half, :] = jnp.where(even, both[C:], both[:C]).astype(jnp.bfloat16)
            yield
        query_grad = query_grad * scale
        for h in range(group):
            place = (group * p + h) * HEAD
            dq_ref[:, place:place + HEAD] = query_grad[h * tokens:(h + 1) * tokens].astype(jnp.bfloat16)

    state = {}
    for p in range(pairs + 1):
        passes = []
        if p > 0:
            passes.append(second_pass(p - 1, state))
        if p < pairs:
            passes.append(first_pass(p, state))
        while passes:
            for one in list(passes):
                if next(one, passes) is passes:
                    passes.remove(one)


def attend(core, q, k, v, sk, sv, g):
    tokens = q.shape[0]
    heads = q.shape[1] // HEAD
    prompt = k.shape[0]
    rows = prompt + tokens

    def whole(*shape):
        return pl.BlockSpec(shape, lambda i, core: (0, 0))

    paired = whole(tokens, heads * HEAD)
    return pl.pallas_call(
        attend_kernel,
        grid_spec=pltpu.PrefetchScalarGridSpec(
            num_scalar_prefetch=1,
            grid=(1,),
            in_specs=[
                paired, paired, whole(prompt, HEAD), whole(prompt, HEAD),
                whole(tokens, HEAD), whole(tokens, HEAD),
            ],
            out_specs=[
                paired, whole(tokens, 2 * HEAD), whole(prompt // 2, 2 * HEAD),
                whole(prompt // 2, 2 * HEAD),
            ],
            scratch_shapes=[
                pltpu.VMEM((heads // 2, rows, 2 * tokens), jnp.float32),
                pltpu.VMEM((heads // 2, rows, 2 * tokens), jnp.float32),
                pltpu.VMEM((rows, HEAD), jnp.float32),
                pltpu.VMEM((rows, HEAD), jnp.float32),
            ],
        ),
        out_shape=[
            jax.ShapeDtypeStruct(q.shape, jnp.bfloat16),
            jax.ShapeDtypeStruct((tokens, 2 * HEAD), jnp.bfloat16),
            jax.ShapeDtypeStruct((prompt // 2, 2 * HEAD), jnp.bfloat16),
            jax.ShapeDtypeStruct((prompt // 2, 2 * HEAD), jnp.bfloat16),
        ],
        compiler_params=pltpu.CompilerParams(vmem_limit_bytes=62 * 1024 * 1024),
        cost_estimate=pl.CostEstimate(
            flops=10 * rows * heads * tokens * HEAD,
            bytes_accessed=4 * 1024 * 1024,
            transcendentals=rows * heads * tokens,
        ),
    )(core, q, g, k, v, sk, sv)


D = 5120
epsilon = 1e-06
RESP = 32
HEADS = 8
CORE_SWAP = [(i, i ^ 1) for i in range(RESP)]
FAR_SWAP = [(i, i ^ 16) for i in range(RESP)]
SAME_CORE = [[2 * i + c for i in range(RESP // 2)] for c in range(2)]
NEAR_SWAP = [(i, i ^ 4) for i in range(HEADS)]
UP = [(i, i // 4 * 4 + (i + 1) % 4) for i in range(HEADS)]
DOWN = [(i, i // 4 * 4 + (i + 3) % 4) for i in range(HEADS)]
EXTRA = 16
SMEM = pl.BlockSpec(memory_space=pltpu.SMEM)
BIG_VMEM = pltpu.CompilerParams(vmem_limit_bytes=62 * 1024 * 1024)


def cost(read, flops=0):
    return pl.CostEstimate(flops=flops, bytes_accessed=read, transcendentals=0)


def pack_kernel(upper_ref, lower_ref, upper_gain_ref, lower_gain_ref, out_ref):
    rows, width = upper_ref.shape
    place = lax.broadcasted_iota(jnp.int32, (EXTRA, width), 0)
    upper_gain = upper_gain_ref[...].astype(jnp.float32).reshape(1, width)
    lower_gain = lower_gain_ref[...].astype(jnp.float32).reshape(1, width)
    gains = jnp.where(place == 0, upper_gain, jnp.where(place == 1, lower_gain, 0.0))
    out_ref[:rows, :] = upper_ref[...]
    out_ref[rows : 2 * rows, :] = lower_ref[...]
    out_ref[2 * rows :, :] = gains.astype(jnp.bfloat16)


def pack(upper_input, lower_input, upper_gain, lower_gain):
    rows, width = upper_input.shape
    return pl.pallas_call(
        pack_kernel,
        out_shape=jax.ShapeDtypeStruct((2 * rows + EXTRA, width), jnp.bfloat16),
        compiler_params=BIG_VMEM,
        cost_estimate=cost(400000),
    )(upper_input, lower_input, upper_gain, lower_gain)


def split_kernel(far_ref, mine_ref, got_ref, own_ref, near_ref, kept_ref, sent_ref, both_ref):
    half = kept_ref.shape[1]
    low = far_ref[0] == 0
    for i in range(kept_ref.shape[0]):
        start = i * 2 * half
        one = mine_ref[start : start + half, :].astype(jnp.float32) + got_ref[
            start : start + half, :
        ].astype(jnp.float32)
        two = mine_ref[start + half : start + 2 * half, :].astype(jnp.float32) + got_ref[
            start + half : start + 2 * half, :
        ].astype(jnp.float32)
        kept_ref[i] = jnp.where(low, one, two).astype(jnp.bfloat16)
        sent_ref[i] = jnp.where(low, two, one).astype(jnp.bfloat16)
    both_ref[0] = own_ref[...]
    both_ref[1] = near_ref[...]


def split(far, mine, got, own, near):
    blocks = RESP // 2
    half = jax.ShapeDtypeStruct((blocks, mine.shape[0] // blocks // 2, mine.shape[1]), mine.dtype)
    vmem = pl.BlockSpec(memory_space=pltpu.VMEM)
    return pl.pallas_call(
        split_kernel,
        in_specs=[SMEM, vmem, vmem, vmem, vmem],
        out_shape=[half, half, jax.ShapeDtypeStruct((2,) + own.shape, own.dtype)],
        compiler_params=BIG_VMEM,
        cost_estimate=cost(3000000),
    )(far, mine, got, own, near)


def join_kernel(kept_ref, far_ref, mine_ref, got_ref, out_ref):
    half = kept_ref.shape[1]
    for i in range(kept_ref.shape[0]):
        part = slice(i * 2 * half, (i + 1) * 2 * half)
        upper = kept_ref[i].astype(jnp.float32) + far_ref[i].astype(jnp.float32)
        lower = mine_ref[part, :].astype(jnp.float32) + got_ref[part, :].astype(jnp.float32)
        out_ref[i, :half, :] = upper.astype(jnp.bfloat16)
        out_ref[i, half:, :] = lower.astype(jnp.bfloat16)


def join(kept, far, mine, got):
    blocks, half, width = kept.shape
    return pl.pallas_call(
        join_kernel,
        out_shape=jax.ShapeDtypeStruct((blocks, 3 * half, width), kept.dtype),
        compiler_params=BIG_VMEM,
        cost_estimate=cost(3000000),
    )(kept, far, mine, got)


def project_kernel(head_ref, blocks_ref, *refs):
    weight_refs = refs[:4]
    piece_refs = refs[4:8]
    out_ref, scaled = refs[8:]
    count, rows, width = out_ref.shape
    half = rows // 2
    sources = blocks_ref.shape[0]

    def total(first, last, part):
        summed = blocks_ref[first, part, :].astype(jnp.float32)
        for i in range(first + 1, last):
            summed = summed + blocks_ref[i, part, :].astype(jnp.float32)
        return summed.astype(jnp.bfloat16)

    upper = jnp.concatenate(
        [
            total(0, sources // 2, slice(0, half)),
            total(sources // 2, sources, slice(0, half)),
        ],
        axis=0,
    )
    lower = total(0, sources, slice(half, 3 * half))
    near = lax.div(head_ref[0], 4)
    across = lax.rem(head_ref[0], 4)
    pieces = []
    for piece_ref, shift in zip(piece_refs, (0, 3, 1, 2)):
        for j in range(2):
            side = near if j == 0 else 1 - near
            pieces.append((piece_ref, j, side * 4 + lax.rem(across + shift, 4)))
    stats = [[jnp.zeros((rows, 1), jnp.float32)] * 2 for layer in range(2)]
    for piece_ref, j, owner in pieces:
        columns = pl.ds(pl.multiple_of(owner * width, 128), width)
        gains = piece_ref[j, 2 * rows :, :].astype(jnp.float32)
        for layer, rounded in enumerate((upper, lower)):
            key_weight = weight_refs[2 * layer][columns, :]
            value_weight = weight_refs[2 * layer + 1][columns, :]
            projected = lax.dot_general(
                rounded[:, :HEAD], key_weight, NT, preferred_element_type=jnp.float32
            ) + lax.dot_general(
                rounded[:, HEAD:], value_weight, NT, preferred_element_type=jnp.float32
            )
            hidden = piece_ref[j, layer * rows : (layer + 1) * rows, :].astype(jnp.float32)
            one = projected * gains[layer : layer + 1]
            scaled[layer, owner] = one
            squares, sums = stats[layer]
            stats[layer] = [
                squares + jnp.sum(hidden * hidden, axis=1, keepdims=True),
                sums + jnp.sum(one * hidden, axis=1, keepdims=True),
            ]
    inverses = []
    shrinks = []
    for squares, sums in stats:
        inverse = lax.rsqrt(squares / D + epsilon)
        inverses.append(inverse)
        shrinks.append(inverse * inverse * inverse * sums / D)
    for piece_ref, j, owner in pieces:
        part = jnp.zeros((rows, width), jnp.float32)
        for layer in range(2):
            hidden = piece_ref[j, layer * rows : (layer + 1) * rows, :].astype(jnp.float32)
            part = part + inverses[layer] * scaled[layer, owner] - shrinks[layer] * hidden
        out_ref[owner] = part.astype(jnp.bfloat16)


def project(head, blocks, weights, pieces):
    rows = blocks.shape[1] // 3 * 2
    width = pieces[0].shape[2]
    vmem = pl.BlockSpec(memory_space=pltpu.VMEM)
    return pl.pallas_call(
        project_kernel,
        in_specs=[SMEM] + [vmem] * 9,
        out_shape=jax.ShapeDtypeStruct((HEADS, rows, width), jnp.bfloat16),
        scratch_shapes=[pltpu.VMEM((2, HEADS, rows, width), jnp.float32)],
        compiler_params=BIG_VMEM,
        cost_estimate=cost(8000000, 8 * rows * D * HEAD),
    )(head, blocks, *weights, *pieces)


def body(
    upper_input, upper_gain, upper_key_weight, upper_value_weight, upper_prompt_keys,
    upper_prompt_values, upper_queries, upper_span_keys, upper_span_values, upper_out_grad,
    lower_input, lower_gain, lower_key_weight, lower_value_weight, lower_prompt_keys,
    lower_prompt_values, lower_queries, lower_span_keys, lower_span_values, lower_out_grad,
):
    place = lax.axis_index("resp").astype(jnp.int32)
    core = lax.rem(place, 2).reshape(1)
    far = lax.div(place, 16).reshape(1)
    head = lax.axis_index("head").astype(jnp.int32).reshape(1)
    own = pack(upper_input, lower_input, upper_gain, lower_gain)
    own, upper_queries = lax.optimization_barrier((own, upper_queries))
    near = lax.ppermute(own, "head", NEAR_SWAP)
    upper_query, upper_span, mine, other = attend(
        core, upper_queries, upper_prompt_keys, upper_prompt_values, upper_span_keys,
        upper_span_values, upper_out_grad,
    )
    other, near = lax.optimization_barrier((other, near))
    got = lax.ppermute(other, "resp", CORE_SWAP)
    kept, sent, pair = split(far, mine, got, own, near)
    sent, pair, lower_queries = lax.optimization_barrier((sent, pair, lower_queries))
    from_far = lax.ppermute(sent, "resp", FAR_SWAP)
    from_below = lax.ppermute(pair, "head", UP)
    from_above = lax.ppermute(pair, "head", DOWN)
    lower_query, lower_span, mine, other = attend(
        core, lower_queries, lower_prompt_keys, lower_prompt_values, lower_span_keys,
        lower_span_values, lower_out_grad,
    )
    other, from_far, from_below, from_above = lax.optimization_barrier(
        (other, from_far, from_below, from_above)
    )
    got = lax.ppermute(other, "resp", CORE_SWAP)
    partial = join(kept, from_far, mine, got)
    from_across = lax.ppermute(from_below, "head", UP)
    blocks = lax.all_to_all(partial, "resp", 0, 0, axis_index_groups=SAME_CORE)
    part = project(
        head,
        blocks,
        (upper_key_weight, upper_value_weight, lower_key_weight, lower_value_weight),
        (pair, from_below, from_above, from_across),
    )
    blocks = lax.all_to_all(part, "head", 0, 0)
    prompt_grads = jnp.sum(blocks.astype(jnp.float32), axis=0).astype(jnp.bfloat16)
    return (upper_query, lower_query, upper_span, lower_span, prompt_grads)


def solution(mesh):
    layer = (
        P("resp", "head"), P("head"), P(None, "head"), P(None, "head"), P(None, "head"),
        P(None, "head"), P("resp", "head"), P("resp", "head"), P("resp", "head"), P("resp", "head"),
    )
    return jax.shard_map(
        body,
        mesh=mesh,
        in_specs=layer + layer,
        out_specs=(P("resp", "head"),) * 5,
        check_vma=False,
    )
```

```python
import functools
import jax
import jax.numpy as jnp
from jax import lax
from jax.experimental import pallas as pl
from jax.experimental.pallas import tpu as pltpu
from jax.sharding import PartitionSpec as P

HEAD = 128
C = 64
NT = (((1,), (1,)), ((), ()))
LAG = 6
TN = (((0,), (0,)), ((), ()))


def attend_kernel(core_ref, q_hbm, g_hbm, k_hbm, v_hbm, sk_hbm, sv_hbm, slopes_hbm, span_hbm,
                  mine_hbm, other_hbm, scores, dots, key_sums, value_sums,
                  q_ref, g_ref, k_ref, v_ref, sk_ref, sv_ref, sems,
                  slopes_ref, span_ref, mine_ref, other_ref, out_sems):
    copies = [
        pltpu.make_async_copy(source, target, sems.at[i])
        for i, (source, target) in enumerate((
            (q_hbm, q_ref), (k_hbm, k_ref), (sk_hbm, sk_ref), (g_hbm, g_ref), (v_hbm, v_ref),
            (sv_hbm, sv_ref),
        ))
    ]
    for copy in copies:
        copy.start()
    for copy in copies[:2]:
        copy.wait()
    tokens = q_ref.shape[0]
    prompt = k_ref.shape[0]
    group = 2
    pair = group * tokens
    pairs = q_ref.shape[1] // (group * HEAD)
    scale = HEAD ** -0.5
    factor = scale * 1.4426950408889634
    chunk = 2 * C
    count = prompt // chunk + 1
    parts = [slice(j * chunk, (j + 1) * chunk) for j in range(count)]
    even = core_ref[0] == 0

    def rows_of(ref, span, j):
        return ref[parts[j], :] if j < count - 1 else span[...]

    def stacked(ref, p):
        heads = [ref[:, h * HEAD:(h + 1) * HEAD] for h in range(group * p, group * p + group)]
        return jnp.concatenate(heads, axis=0)

    def first_pass(p, state):
        query = stacked(q_ref, p)
        grad = None if p == 0 else stacked(g_ref, p)
        tops = []
        totals = []
        deltas = []
        for j in range(count):
            block = lax.dot_general(
                rows_of(k_ref, sk_ref, j), query, NT, preferred_element_type=jnp.float32
            )
            if j == count - 1:
                u = lax.broadcasted_iota(jnp.int32, block.shape, 0)
                t = lax.rem(lax.broadcasted_iota(jnp.int32, block.shape, 1), tokens)
                block = jnp.where((lax.div(u, C) == lax.div(t, C)) & (u <= t), block, -1e30)
            top = jnp.max(block, axis=0, keepdims=True)
            block = jnp.exp2((block - top) * factor)
            scores[p, parts[j], :] = block
            if grad is None:
                for copy in copies[2:]:
                    copy.wait()
                grad = stacked(g_ref, p)
            dot = lax.dot_general(
                rows_of(v_ref, sv_ref, j), grad, NT, preferred_element_type=jnp.float32
            )
            dots[p, parts[j], :] = dot
            tops.append(top)
            totals.append(jnp.sum(block, axis=0, keepdims=True))
            deltas.append(jnp.sum(block * dot, axis=0, keepdims=True))
            yield
        tops = jnp.concatenate(tops, axis=0)
        weigh = jnp.exp2((tops - jnp.max(tops, axis=0, keepdims=True)) * factor)
        total = jnp.sum(weigh * jnp.concatenate(totals, axis=0), axis=0, keepdims=True)
        weigh = weigh / total
        delta = jnp.sum(weigh * jnp.concatenate(deltas, axis=0), axis=0, keepdims=True)
        state[p] = (query, grad, weigh, delta)

    def second_pass(p, state):
        query, grad, weigh, delta = state.pop(p)
        for j in range(count):
            weight = scores[p, parts[j], :] * weigh[j:j + 1, :]
            slope = (weight * (dots[p, parts[j], :] - delta)).astype(jnp.bfloat16)
            weight = weight.astype(jnp.bfloat16)
            slopes_ref[p, parts[j], :] = slope
            key_sum = jnp.dot(slope, query, preferred_element_type=jnp.float32)
            value_sum = jnp.dot(weight, grad, preferred_element_type=jnp.float32)
            if p > 0:
                key_sum = key_sum + key_sums[parts[j], :]
                value_sum = value_sum + value_sums[parts[j], :]
            if p < pairs - 1:
                key_sums[parts[j], :] = key_sum
                value_sums[parts[j], :] = value_sum
            else:
                both = jnp.concatenate([key_sum * scale, value_sum], axis=1)
                if j == count - 1:
                    span_ref[...] = both.astype(jnp.bfloat16)
                    send(span_ref, span_hbm)
                else:
                    half = slice(j * C, (j + 1) * C)
                    mine_ref[half, :] = jnp.where(even, both[:C], both[C:]).astype(jnp.bfloat16)
                    other_ref[half, :] = jnp.where(even, both[C:], both[:C]).astype(jnp.bfloat16)
                    if j % 4 == 3:
                        ready = slice((j - 3) * C, (j + 1) * C)
                        send(other_ref.at[ready, :], other_hbm.at[ready, :])
                        send(mine_ref.at[ready, :], mine_hbm.at[ready, :])
            yield
        send(slopes_ref.at[p], slopes_hbm.at[p])

    outs = []

    def send(source, target):
        copy = pltpu.make_async_copy(source, target, out_sems.at[len(outs)])
        copy.start()
        outs.append(copy)

    state = {}

    def chained(one):
        for p in range(pairs):
            yield from one(p, state)

    first = chained(first_pass)
    second = chained(second_pass)
    for ahead in range(count + LAG):
        next(first)
    for unused in second:
        next(first, None)
    for copy in outs:
        copy.wait()


def attend(core, q, k, v, sk, sv, g):
    tokens = q.shape[0]
    heads = q.shape[1] // HEAD
    prompt = k.shape[0]
    rows = prompt + tokens

    def whole(*shape):
        return pl.BlockSpec(shape, lambda i, core: (0, 0))

    paired = whole(tokens, heads * HEAD)
    return pl.pallas_call(
        attend_kernel,
        grid_spec=pltpu.PrefetchScalarGridSpec(
            num_scalar_prefetch=1,
            grid=(1,),
            in_specs=[
                pl.BlockSpec(memory_space=pl.ANY)
            ] * 6,
            out_specs=[pl.BlockSpec(memory_space=pl.ANY)] * 4,
            scratch_shapes=[
                pltpu.VMEM((heads // 2, rows, 2 * tokens), jnp.float32),
                pltpu.VMEM((heads // 2, rows, 2 * tokens), jnp.float32),
                pltpu.VMEM((rows, HEAD), jnp.float32),
                pltpu.VMEM((rows, HEAD), jnp.float32),
                pltpu.VMEM(q.shape, jnp.bfloat16),
                pltpu.VMEM(g.shape, jnp.bfloat16),
                pltpu.VMEM(k.shape, jnp.bfloat16),
                pltpu.VMEM(v.shape, jnp.bfloat16),
                pltpu.VMEM(sk.shape, jnp.bfloat16),
                pltpu.VMEM(sv.shape, jnp.bfloat16),
                pltpu.SemaphoreType.DMA((6,)),
                pltpu.VMEM((heads // 2, rows, 2 * tokens), jnp.bfloat16),
                pltpu.VMEM((tokens, 2 * HEAD), jnp.bfloat16),
                pltpu.VMEM((prompt // 2, 2 * HEAD), jnp.bfloat16),
                pltpu.VMEM((prompt // 2, 2 * HEAD), jnp.bfloat16),
                pltpu.SemaphoreType.DMA((13,)),
            ],
        ),
        out_shape=[
            jax.ShapeDtypeStruct((heads // 2, rows, 2 * tokens), jnp.bfloat16),
            jax.ShapeDtypeStruct((tokens, 2 * HEAD), jnp.bfloat16),
            jax.ShapeDtypeStruct((prompt // 2, 2 * HEAD), jnp.bfloat16),
            jax.ShapeDtypeStruct((prompt // 2, 2 * HEAD), jnp.bfloat16),
        ],
        compiler_params=pltpu.CompilerParams(vmem_limit_bytes=62 * 1024 * 1024),
        cost_estimate=pl.CostEstimate(
            flops=10 * rows * heads * tokens * HEAD,
            bytes_accessed=4 * 1024 * 1024,
            transcendentals=rows * heads * tokens,
        ),
    )(core, q, g, k, v, sk, sv)


def query_kernel(slopes_ref, k_ref, sk_ref, dq_ref):
    prompt = k_ref.shape[0]
    tokens = dq_ref.shape[0]
    sums = lax.dot_general(
        slopes_ref[0, :prompt, :], k_ref[...], TN, preferred_element_type=jnp.float32
    ) + lax.dot_general(
        slopes_ref[0, prompt:, :], sk_ref[...], TN, preferred_element_type=jnp.float32
    )
    sums = (sums * HEAD ** -0.5).astype(jnp.bfloat16)
    dq_ref[:, :HEAD] = sums[:tokens]
    dq_ref[:, HEAD:] = sums[tokens:]


def query_grads(slopes, k, sk):
    pairs, rows, width = slopes.shape
    tokens = sk.shape[0]
    return pl.pallas_call(
        query_kernel,
        grid=(pairs,),
        in_specs=[
            pl.BlockSpec((1, rows, width), lambda i: (i, 0, 0)),
            pl.BlockSpec(k.shape, lambda i: (0, 0)),
            pl.BlockSpec(sk.shape, lambda i: (0, 0)),
        ],
        out_specs=pl.BlockSpec((tokens, width), lambda i: (0, i)),
        out_shape=jax.ShapeDtypeStruct((tokens, pairs * width), jnp.bfloat16),
        compiler_params=pltpu.CompilerParams(vmem_limit_bytes=62 * 1024 * 1024),
        cost_estimate=pl.CostEstimate(
            flops=2 * pairs * rows * width * HEAD,
            bytes_accessed=6 * 1024 * 1024,
            transcendentals=0,
        ),
    )(slopes, k, sk)


D = 5120
epsilon = 1e-06
RESP = 32
HEADS = 8
CORE_SWAP = [(i, i ^ 1) for i in range(RESP)]
FAR_SWAP = [(i, i ^ 16) for i in range(RESP)]
SAME_CORE = [[2 * i + c for i in range(RESP // 2)] for c in range(2)]
NEAR_SWAP = [(i, i ^ 4) for i in range(HEADS)]
UP = [(i, i // 4 * 4 + (i + 1) % 4) for i in range(HEADS)]
DOWN = [(i, i // 4 * 4 + (i + 3) % 4) for i in range(HEADS)]
EXTRA = 16
SMEM = pl.BlockSpec(memory_space=pltpu.SMEM)
BIG_VMEM = pltpu.CompilerParams(vmem_limit_bytes=62 * 1024 * 1024)


def cost(read, flops=0):
    return pl.CostEstimate(flops=flops, bytes_accessed=read, transcendentals=0)


def pack_kernel(upper_ref, lower_ref, upper_gain_ref, lower_gain_ref, out_ref):
    rows, width = upper_ref.shape
    place = lax.broadcasted_iota(jnp.int32, (EXTRA, width), 0)
    upper_gain = upper_gain_ref[...].astype(jnp.float32).reshape(1, width)
    lower_gain = lower_gain_ref[...].astype(jnp.float32).reshape(1, width)
    gains = jnp.where(place == 0, upper_gain, jnp.where(place == 1, lower_gain, 0.0))
    out_ref[:rows, :] = upper_ref[...]
    out_ref[rows : 2 * rows, :] = lower_ref[...]
    out_ref[2 * rows :, :] = gains.astype(jnp.bfloat16)


def pack(upper_input, lower_input, upper_gain, lower_gain):
    rows, width = upper_input.shape
    return pl.pallas_call(
        pack_kernel,
        out_shape=jax.ShapeDtypeStruct((2 * rows + EXTRA, width), jnp.bfloat16),
        compiler_params=BIG_VMEM,
        cost_estimate=cost(400000),
    )(upper_input, lower_input, upper_gain, lower_gain)


def split(far, mine, got):
    total = mine.astype(jnp.float32) + got.astype(jnp.float32)
    total = total.astype(jnp.bfloat16).reshape(RESP // 2, 2, -1, mine.shape[1])
    low = far == 0
    kept = jnp.where(low, total[:, 0], total[:, 1])
    sent = jnp.where(low, total[:, 1], total[:, 0])
    return kept, sent


def join(kept, far, mine, got):
    upper = (kept.astype(jnp.float32) + far.astype(jnp.float32)).astype(jnp.bfloat16)
    lower = (mine.astype(jnp.float32) + got.astype(jnp.float32)).astype(jnp.bfloat16)
    return jnp.concatenate([upper, lower.reshape(RESP // 2, -1, mine.shape[1])], axis=1)


def project_kernel(head_ref, blocks_ref, *refs):
    piece_refs = refs[:8]
    weight_hbm = refs[8:12]
    out_ref, weights_ref, scaled, sems = refs[12:]
    count, rows, width = out_ref.shape
    half = rows // 2
    sources = blocks_ref.shape[0]
    copies = [
        pltpu.make_async_copy(
            source, weights_ref.at[w // 2, :, pl.ds(w % 2 * HEAD, HEAD)], sems.at[w]
        )
        for w, source in enumerate(weight_hbm)
    ]
    for copy in copies:
        copy.start()

    def total(first, last, part):
        summed = blocks_ref[first, part, :].astype(jnp.float32)
        for i in range(first + 1, last):
            summed = summed + blocks_ref[i, part, :].astype(jnp.float32)
        return summed.astype(jnp.bfloat16)

    upper = jnp.concatenate(
        [
            total(0, sources // 2, slice(0, half)),
            total(sources // 2, sources, slice(0, half)),
        ],
        axis=0,
    )
    lower = total(0, sources, slice(half, 3 * half))
    near = lax.div(head_ref[0], 4)
    across = lax.rem(head_ref[0], 4)
    owners = []
    for shift in (0, 3, 1, 2):
        for side in (near, 1 - near):
            owners.append(side * 4 + lax.rem(across + shift, 4))
    inverses = []
    shrinks = []
    groups = width // 128

    def folded(values):
        return sum(values[:, g * 128 : (g + 1) * 128] for g in range(groups))

    for layer, rounded in enumerate((upper, lower)):
        place = slice(layer * rows, (layer + 1) * rows)
        squares = jnp.zeros((rows, 128), jnp.float32)
        sums = jnp.zeros((rows, 128), jnp.float32)
        for piece_ref in piece_refs:
            hidden = piece_ref[place, :].astype(jnp.float32)
            squares = squares + folded(hidden * hidden)
        for copy in copies[2 * layer : 2 * layer + 2]:
            copy.wait()
        for i, (piece_ref, owner) in enumerate(zip(piece_refs, owners)):
            columns = pl.ds(pl.multiple_of(owner * width, 128), width)
            gains = piece_ref[2 * rows :, :].astype(jnp.float32)
            projected = lax.dot_general(
                rounded, weights_ref[layer, columns, :], NT, preferred_element_type=jnp.float32
            )
            one = projected * gains[layer : layer + 1]
            scaled[layer, i] = one
            sums = sums + folded(one * piece_ref[place, :].astype(jnp.float32))
        squares = jnp.sum(squares, axis=1, keepdims=True)
        sums = jnp.sum(sums, axis=1, keepdims=True)
        inverse = lax.rsqrt(squares / D + epsilon)
        inverses.append(inverse)
        shrinks.append(inverse * inverse * inverse * sums / D)
    for i, (piece_ref, owner) in enumerate(zip(piece_refs, owners)):
        part = jnp.zeros((rows, width), jnp.float32)
        for layer in range(2):
            hidden = piece_ref[layer * rows : (layer + 1) * rows, :].astype(jnp.float32)
            part = part + inverses[layer] * scaled[layer, i] - shrinks[layer] * hidden
        out_ref[owner] = part.astype(jnp.bfloat16)


def project(head, blocks, weights, pieces):
    rows = blocks.shape[1] // 3 * 2
    width = pieces[0].shape[1]
    vmem = pl.BlockSpec(memory_space=pltpu.VMEM)
    return pl.pallas_call(
        project_kernel,
        in_specs=[SMEM] + [vmem] * 9 + [pl.BlockSpec(memory_space=pl.ANY)] * 4,
        out_specs=vmem,
        out_shape=jax.ShapeDtypeStruct((HEADS, rows, width), jnp.bfloat16),
        scratch_shapes=[
            pltpu.VMEM((2, D, 2 * HEAD), jnp.bfloat16),
            pltpu.VMEM((2, HEADS, rows, width), jnp.float32),
            pltpu.SemaphoreType.DMA((4,)),
        ],
        compiler_params=pltpu.CompilerParams(vmem_limit_bytes=58 * 1024 * 1024),
        cost_estimate=cost(8000000, 8 * rows * D * HEAD),
    )(head, blocks, *pieces, *weights)


def body(
    upper_input, upper_gain, upper_key_weight, upper_value_weight, upper_prompt_keys,
    upper_prompt_values, upper_queries, upper_span_keys, upper_span_values, upper_out_grad,
    lower_input, lower_gain, lower_key_weight, lower_value_weight, lower_prompt_keys,
    lower_prompt_values, lower_queries, lower_span_keys, lower_span_values, lower_out_grad,
):
    place = lax.axis_index("resp").astype(jnp.int32)
    core = lax.rem(place, 2).reshape(1)
    far = lax.div(place, 16)
    head = lax.axis_index("head").astype(jnp.int32).reshape(1)
    own = pack(upper_input, lower_input, upper_gain, lower_gain)
    own, upper_queries = lax.optimization_barrier((own, upper_queries))
    near = lax.ppermute(own, "head", NEAR_SWAP)
    upper_slopes, upper_span, mine, other = attend(
        core, upper_queries, upper_prompt_keys, upper_prompt_values, upper_span_keys,
        upper_span_values, upper_out_grad,
    )
    other, near = lax.optimization_barrier((other, near))
    got = lax.ppermute(other, "resp", CORE_SWAP)
    kept, sent = split(far, mine, got)
    sent, own, near, lower_queries = lax.optimization_barrier((sent, own, near, lower_queries))
    from_far = lax.ppermute(sent, "resp", FAR_SWAP)
    below = [lax.ppermute(one, "head", UP) for one in (own, near)]
    lower_slopes, lower_span, mine, other = attend(
        core, lower_queries, lower_prompt_keys, lower_prompt_values, lower_span_keys,
        lower_span_values, lower_out_grad,
    )
    other, from_far, below = lax.optimization_barrier((other, from_far, below))
    got = lax.ppermute(other, "resp", CORE_SWAP)
    partial = join(kept, from_far, mine, got)
    partial, own, near, below, upper_slopes = lax.optimization_barrier(
        (partial, own, near, below, upper_slopes)
    )
    across = [lax.ppermute(one, "head", UP) for one in below]
    above = [lax.ppermute(one, "head", DOWN) for one in (own, near)]
    blocks = lax.all_to_all(partial, "resp", 0, 0, axis_index_groups=SAME_CORE)
    upper_query = query_grads(upper_slopes, upper_prompt_keys, upper_span_keys)
    blocks, upper_query = lax.optimization_barrier((blocks, upper_query))
    part = project(
        head,
        blocks,
        (upper_key_weight, upper_value_weight, lower_key_weight, lower_value_weight),
        (own, near, *below, *above, *across),
    )
    part, lower_slopes = lax.optimization_barrier((part, lower_slopes))
    blocks = lax.all_to_all(part, "head", 0, 0)
    lower_query = query_grads(lower_slopes, lower_prompt_keys, lower_span_keys)
    prompt_grads = jnp.sum(blocks.astype(jnp.float32), axis=0).astype(jnp.bfloat16)
    return (upper_query, lower_query, upper_span, lower_span, prompt_grads)


def solution(mesh):
    layer = (
        P("resp", "head"), P("head"), P(None, "head"), P(None, "head"), P(None, "head"),
        P(None, "head"), P("resp", "head"), P("resp", "head"), P("resp", "head"), P("resp", "head"),
    )
    return jax.shard_map(
        body,
        mesh=mesh,
        in_specs=layer + layer,
        out_specs=(P("resp", "head"),) * 5,
        check_vma=False,
    )
```

```python
import functools
import jax
import jax.numpy as jnp
from jax import lax
from jax.experimental import pallas as pl
from jax.experimental.pallas import tpu as pltpu
from jax.sharding import PartitionSpec as P

HEAD = 128
C = 64
NT = (((1,), (1,)), ((), ()))
LAG = 6
TN = (((0,), (0,)), ((), ()))


def attend_kernel(core_ref, q_hbm, g_hbm, k_hbm, v_hbm, sk_hbm, sv_hbm, slopes_hbm, span_hbm,
                  mine_hbm, other_hbm, scores, dots, key_sums, value_sums,
                  q_ref, g_ref, k_ref, v_ref, sk_ref, sv_ref, sems,
                  slopes_ref, span_ref, mine_ref, other_ref, out_sems):
    copies = [
        pltpu.make_async_copy(source, target, sems.at[i])
        for i, (source, target) in enumerate((
            (q_hbm, q_ref), (k_hbm, k_ref), (sk_hbm, sk_ref), (g_hbm, g_ref), (v_hbm, v_ref),
            (sv_hbm, sv_ref),
        ))
    ]
    for copy in copies:
        copy.start()
    for copy in copies[:2]:
        copy.wait()
    tokens = q_ref.shape[0]
    prompt = k_ref.shape[0]
    group = 2
    pair = group * tokens
    pairs = q_ref.shape[1] // (group * HEAD)
    scale = HEAD ** -0.5
    factor = scale * 1.4426950408889634
    chunk = 2 * C
    count = prompt // chunk + 1
    parts = [slice(j * chunk, (j + 1) * chunk) for j in range(count)]
    even = core_ref[0] == 0

    def rows_of(ref, span, j):
        return ref[parts[j], :] if j < count - 1 else span[...]

    def stacked(ref, p):
        heads = [ref[:, h * HEAD:(h + 1) * HEAD] for h in range(group * p, group * p + group)]
        return jnp.concatenate(heads, axis=0)

    def first_pass(p, state):
        query = stacked(q_ref, p)
        grad = None if p == 0 else stacked(g_ref, p)
        tops = []
        totals = []
        deltas = []
        for j in range(count):
            block = lax.dot_general(
                rows_of(k_ref, sk_ref, j), query, NT, preferred_element_type=jnp.float32
            )
            if j == count - 1:
                u = lax.broadcasted_iota(jnp.int32, block.shape, 0)
                t = lax.rem(lax.broadcasted_iota(jnp.int32, block.shape, 1), tokens)
                block = jnp.where((lax.div(u, C) == lax.div(t, C)) & (u <= t), block, -1e30)
            top = jnp.max(block, axis=0, keepdims=True)
            block = jnp.exp2((block - top) * factor)
            scores[p, parts[j], :] = block
            if grad is None:
                for copy in copies[2:]:
                    copy.wait()
                grad = stacked(g_ref, p)
            dot = lax.dot_general(
                rows_of(v_ref, sv_ref, j), grad, NT, preferred_element_type=jnp.float32
            )
            dots[p, parts[j], :] = dot
            tops.append(top)
            totals.append(jnp.sum(block, axis=0, keepdims=True))
            deltas.append(jnp.sum(block * dot, axis=0, keepdims=True))
            yield
        tops = jnp.concatenate(tops, axis=0)
        weigh = jnp.exp2((tops - jnp.max(tops, axis=0, keepdims=True)) * factor)
        total = jnp.sum(weigh * jnp.concatenate(totals, axis=0), axis=0, keepdims=True)
        weigh = weigh / total
        delta = jnp.sum(weigh * jnp.concatenate(deltas, axis=0), axis=0, keepdims=True)
        state[p] = (query, grad, weigh, delta)

    def second_pass(p, state):
        query, grad, weigh, delta = state.pop(p)
        for j in range(count):
            weight = scores[p, parts[j], :] * weigh[j:j + 1, :]
            slope = (weight * (dots[p, parts[j], :] - delta)).astype(jnp.bfloat16)
            weight = weight.astype(jnp.bfloat16)
            slopes_ref[p, parts[j], :] = slope
            key_sum = jnp.dot(slope, query, preferred_element_type=jnp.float32)
            value_sum = jnp.dot(weight, grad, preferred_element_type=jnp.float32)
            if p > 0:
                key_sum = key_sum + key_sums[parts[j], :]
                value_sum = value_sum + value_sums[parts[j], :]
            if p < pairs - 1:
                key_sums[parts[j], :] = key_sum
                value_sums[parts[j], :] = value_sum
            else:
                both = jnp.concatenate([key_sum * scale, value_sum], axis=1)
                if j == count - 1:
                    span_ref[...] = both.astype(jnp.bfloat16)
                    send(span_ref, span_hbm)
                else:
                    half = slice(j * C, (j + 1) * C)
                    mine_ref[half, :] = jnp.where(even, both[:C], both[C:]).astype(jnp.bfloat16)
                    other_ref[half, :] = jnp.where(even, both[C:], both[:C]).astype(jnp.bfloat16)
                    if j % 4 == 3:
                        ready = slice((j - 3) * C, (j + 1) * C)
                        send(other_ref.at[ready, :], other_hbm.at[ready, :])
                        send(mine_ref.at[ready, :], mine_hbm.at[ready, :])
            yield
        send(slopes_ref.at[p], slopes_hbm.at[p])

    outs = []

    def send(source, target):
        copy = pltpu.make_async_copy(source, target, out_sems.at[len(outs)])
        copy.start()
        outs.append(copy)

    state = {}

    def chained(one):
        for p in range(pairs):
            yield from one(p, state)

    first = chained(first_pass)
    second = chained(second_pass)
    for ahead in range(count + LAG):
        next(first)
    for unused in second:
        next(first, None)
    for copy in outs:
        copy.wait()


def attend(core, q, k, v, sk, sv, g):
    tokens = q.shape[0]
    heads = q.shape[1] // HEAD
    prompt = k.shape[0]
    rows = prompt + tokens

    def whole(*shape):
        return pl.BlockSpec(shape, lambda i, core: (0, 0))

    paired = whole(tokens, heads * HEAD)
    return pl.pallas_call(
        attend_kernel,
        grid_spec=pltpu.PrefetchScalarGridSpec(
            num_scalar_prefetch=1,
            grid=(1,),
            in_specs=[
                pl.BlockSpec(memory_space=pl.ANY)
            ] * 6,
            out_specs=[pl.BlockSpec(memory_space=pl.ANY)] * 4,
            scratch_shapes=[
                pltpu.VMEM((heads // 2, rows, 2 * tokens), jnp.float32),
                pltpu.VMEM((heads // 2, rows, 2 * tokens), jnp.float32),
                pltpu.VMEM((rows, HEAD), jnp.float32),
                pltpu.VMEM((rows, HEAD), jnp.float32),
                pltpu.VMEM(q.shape, jnp.bfloat16),
                pltpu.VMEM(g.shape, jnp.bfloat16),
                pltpu.VMEM(k.shape, jnp.bfloat16),
                pltpu.VMEM(v.shape, jnp.bfloat16),
                pltpu.VMEM(sk.shape, jnp.bfloat16),
                pltpu.VMEM(sv.shape, jnp.bfloat16),
                pltpu.SemaphoreType.DMA((6,)),
                pltpu.VMEM((heads // 2, rows, 2 * tokens), jnp.bfloat16),
                pltpu.VMEM((tokens, 2 * HEAD), jnp.bfloat16),
                pltpu.VMEM((prompt // 2, 2 * HEAD), jnp.bfloat16),
                pltpu.VMEM((prompt // 2, 2 * HEAD), jnp.bfloat16),
                pltpu.SemaphoreType.DMA((13,)),
            ],
        ),
        out_shape=[
            jax.ShapeDtypeStruct((heads // 2, rows, 2 * tokens), jnp.bfloat16),
            jax.ShapeDtypeStruct((tokens, 2 * HEAD), jnp.bfloat16),
            jax.ShapeDtypeStruct((prompt // 2, 2 * HEAD), jnp.bfloat16),
            jax.ShapeDtypeStruct((prompt // 2, 2 * HEAD), jnp.bfloat16),
        ],
        compiler_params=pltpu.CompilerParams(vmem_limit_bytes=62 * 1024 * 1024),
        cost_estimate=pl.CostEstimate(
            flops=10 * rows * heads * tokens * HEAD,
            bytes_accessed=4 * 1024 * 1024,
            transcendentals=rows * heads * tokens,
        ),
    )(core, q, g, k, v, sk, sv)


def query_kernel(slopes_ref, k_ref, sk_ref, dq_ref):
    prompt = k_ref.shape[0]
    tokens = dq_ref.shape[0]
    sums = lax.dot_general(
        slopes_ref[0, :prompt, :], k_ref[...], TN, preferred_element_type=jnp.float32
    ) + lax.dot_general(
        slopes_ref[0, prompt:, :], sk_ref[...], TN, preferred_element_type=jnp.float32
    )
    sums = (sums * HEAD ** -0.5).astype(jnp.bfloat16)
    dq_ref[:, :HEAD] = sums[:tokens]
    dq_ref[:, HEAD:] = sums[tokens:]


def query_grads(slopes, k, sk):
    pairs, rows, width = slopes.shape
    tokens = sk.shape[0]
    return pl.pallas_call(
        query_kernel,
        grid=(pairs,),
        in_specs=[
            pl.BlockSpec((1, rows, width), lambda i: (i, 0, 0)),
            pl.BlockSpec(k.shape, lambda i: (0, 0)),
            pl.BlockSpec(sk.shape, lambda i: (0, 0)),
        ],
        out_specs=pl.BlockSpec((tokens, width), lambda i: (0, i)),
        out_shape=jax.ShapeDtypeStruct((tokens, pairs * width), jnp.bfloat16),
        compiler_params=pltpu.CompilerParams(vmem_limit_bytes=62 * 1024 * 1024),
        cost_estimate=pl.CostEstimate(
            flops=2 * pairs * rows * width * HEAD,
            bytes_accessed=6 * 1024 * 1024,
            transcendentals=0,
        ),
    )(slopes, k, sk)


D = 5120
epsilon = 1e-06
RESP = 32
HEADS = 8
CORE_SWAP = [(i, i ^ 1) for i in range(RESP)]
FAR_SWAP = [(i, i ^ 16) for i in range(RESP)]
SAME_CORE = [[2 * i + c for i in range(RESP // 2)] for c in range(2)]
NEAR_SWAP = [(i, i ^ 4) for i in range(HEADS)]
UP = [(i, i // 4 * 4 + (i + 1) % 4) for i in range(HEADS)]
DOWN = [(i, i // 4 * 4 + (i + 3) % 4) for i in range(HEADS)]
ACROSS = [(i, i ^ 2) for i in range(HEADS)]
EXTRA = 16
SMEM = pl.BlockSpec(memory_space=pltpu.SMEM)
BIG_VMEM = pltpu.CompilerParams(vmem_limit_bytes=62 * 1024 * 1024)


def cost(read, flops=0):
    return pl.CostEstimate(flops=flops, bytes_accessed=read, transcendentals=0)


def pack_kernel(upper_ref, lower_ref, upper_gain_ref, lower_gain_ref, out_ref):
    rows, width = upper_ref.shape
    place = lax.broadcasted_iota(jnp.int32, (EXTRA, width), 0)
    upper_gain = upper_gain_ref[...].astype(jnp.float32).reshape(1, width)
    lower_gain = lower_gain_ref[...].astype(jnp.float32).reshape(1, width)
    gains = jnp.where(place == 0, upper_gain, jnp.where(place == 1, lower_gain, 0.0))
    out_ref[:rows, :] = upper_ref[...]
    out_ref[rows : 2 * rows, :] = lower_ref[...]
    out_ref[2 * rows :, :] = gains.astype(jnp.bfloat16)


def pack(upper_input, lower_input, upper_gain, lower_gain):
    rows, width = upper_input.shape
    return pl.pallas_call(
        pack_kernel,
        out_shape=jax.ShapeDtypeStruct((2 * rows + EXTRA, width), jnp.bfloat16),
        compiler_params=BIG_VMEM,
        cost_estimate=cost(400000),
    )(upper_input, lower_input, upper_gain, lower_gain)


def split(far, mine, got):
    total = mine.astype(jnp.float32) + got.astype(jnp.float32)
    total = total.astype(jnp.bfloat16).reshape(RESP // 2, 2, -1, mine.shape[1])
    low = far == 0
    kept = jnp.where(low, total[:, 0], total[:, 1])
    sent = jnp.where(low, total[:, 1], total[:, 0])
    return kept, sent


def join(kept, far, mine, got):
    upper = (kept.astype(jnp.float32) + far.astype(jnp.float32)).astype(jnp.bfloat16)
    lower = (mine.astype(jnp.float32) + got.astype(jnp.float32)).astype(jnp.bfloat16)
    return jnp.concatenate([upper, lower.reshape(RESP // 2, -1, mine.shape[1])], axis=1)


def project_kernel(head_ref, blocks_ref, *refs):
    piece_refs = refs[:8]
    weight_hbm = refs[8:12]
    out_ref, weights_ref, scaled, sems = refs[12:]
    count, rows, width = out_ref.shape
    half = rows // 2
    sources = blocks_ref.shape[0]
    copies = [
        pltpu.make_async_copy(
            source, weights_ref.at[w // 2, :, pl.ds(w % 2 * HEAD, HEAD)], sems.at[w]
        )
        for w, source in enumerate(weight_hbm)
    ]
    for copy in copies:
        copy.start()

    def total(first, last, part):
        summed = blocks_ref[first, part, :].astype(jnp.float32)
        for i in range(first + 1, last):
            summed = summed + blocks_ref[i, part, :].astype(jnp.float32)
        return summed.astype(jnp.bfloat16)

    upper = jnp.concatenate(
        [
            total(0, sources // 2, slice(0, half)),
            total(sources // 2, sources, slice(0, half)),
        ],
        axis=0,
    )
    lower = total(0, sources, slice(half, 3 * half))
    near = lax.div(head_ref[0], 4)
    across = lax.rem(head_ref[0], 4)
    owners = []
    for shift in (0, 3, 1, 2):
        for side in (near, 1 - near):
            owners.append(side * 4 + lax.rem(across + shift, 4))
    inverses = []
    shrinks = []
    groups = width // 128

    def folded(values):
        return sum(values[:, g * 128 : (g + 1) * 128] for g in range(groups))

    for layer, rounded in enumerate((upper, lower)):
        place = slice(layer * rows, (layer + 1) * rows)
        squares = jnp.zeros((rows, 128), jnp.float32)
        sums = jnp.zeros((rows, 128), jnp.float32)
        for piece_ref in piece_refs:
            hidden = piece_ref[place, :].astype(jnp.float32)
            squares = squares + folded(hidden * hidden)
        for copy in copies[2 * layer : 2 * layer + 2]:
            copy.wait()
        for i, (piece_ref, owner) in enumerate(zip(piece_refs, owners)):
            columns = pl.ds(pl.multiple_of(owner * width, 128), width)
            gains = piece_ref[2 * rows :, :].astype(jnp.float32)
            projected = lax.dot_general(
                rounded, weights_ref[layer, columns, :], NT, preferred_element_type=jnp.float32
            )
            one = projected * gains[layer : layer + 1]
            scaled[layer, i] = one
            sums = sums + folded(one * piece_ref[place, :].astype(jnp.float32))
        squares = jnp.sum(squares, axis=1, keepdims=True)
        sums = jnp.sum(sums, axis=1, keepdims=True)
        inverse = lax.rsqrt(squares / D + epsilon)
        inverses.append(inverse)
        shrinks.append(inverse * inverse * inverse * sums / D)
    for i, (piece_ref, owner) in enumerate(zip(piece_refs, owners)):
        part = jnp.zeros((rows, width), jnp.float32)
        for layer in range(2):
            hidden = piece_ref[layer * rows : (layer + 1) * rows, :].astype(jnp.float32)
            part = part + inverses[layer] * scaled[layer, i] - shrinks[layer] * hidden
        out_ref[owner] = part.astype(jnp.bfloat16)


def project(head, blocks, weights, pieces):
    rows = blocks.shape[1] // 3 * 2
    width = pieces[0].shape[1]
    vmem = pl.BlockSpec(memory_space=pltpu.VMEM)
    return pl.pallas_call(
        project_kernel,
        in_specs=[SMEM] + [vmem] * 9 + [pl.BlockSpec(memory_space=pl.ANY)] * 4,
        out_specs=vmem,
        out_shape=jax.ShapeDtypeStruct((HEADS, rows, width), jnp.bfloat16),
        scratch_shapes=[
            pltpu.VMEM((2, D, 2 * HEAD), jnp.bfloat16),
            pltpu.VMEM((2, HEADS, rows, width), jnp.float32),
            pltpu.SemaphoreType.DMA((4,)),
        ],
        compiler_params=pltpu.CompilerParams(vmem_limit_bytes=58 * 1024 * 1024),
        cost_estimate=cost(8000000, 8 * rows * D * HEAD),
    )(head, blocks, *pieces, *weights)


def body(
    upper_input, upper_gain, upper_key_weight, upper_value_weight, upper_prompt_keys,
    upper_prompt_values, upper_queries, upper_span_keys, upper_span_values, upper_out_grad,
    lower_input, lower_gain, lower_key_weight, lower_value_weight, lower_prompt_keys,
    lower_prompt_values, lower_queries, lower_span_keys, lower_span_values, lower_out_grad,
):
    place = lax.axis_index("resp").astype(jnp.int32)
    core = lax.rem(place, 2).reshape(1)
    far = lax.div(place, 16)
    head = lax.axis_index("head").astype(jnp.int32).reshape(1)
    upper_slopes, upper_span, mine, other = attend(
        core, upper_queries, upper_prompt_keys, upper_prompt_values, upper_span_keys,
        upper_span_values, upper_out_grad,
    )
    other, upper_input = lax.optimization_barrier((other, upper_input))
    got = lax.ppermute(other, "resp", CORE_SWAP)
    own = pack(upper_input, lower_input, upper_gain, lower_gain)
    kept, sent = split(far, mine, got)
    sent, own, lower_queries = lax.optimization_barrier((sent, own, lower_queries))
    from_far = lax.ppermute(sent, "resp", FAR_SWAP)
    near = lax.ppermute(own, "head", NEAR_SWAP)
    lower_slopes, lower_span, mine, other = attend(
        core, lower_queries, lower_prompt_keys, lower_prompt_values, lower_span_keys,
        lower_span_values, lower_out_grad,
    )
    other, from_far, near = lax.optimization_barrier((other, from_far, near))
    got = lax.ppermute(other, "resp", CORE_SWAP)
    partial = join(kept, from_far, mine, got)
    partial, own, near, upper_slopes = lax.optimization_barrier((partial, own, near, upper_slopes))
    below = [lax.ppermute(one, "head", UP) for one in (own, near)]
    across = [lax.ppermute(one, "head", ACROSS) for one in (own, near)]
    above = [lax.ppermute(one, "head", DOWN) for one in (own, near)]
    blocks = lax.all_to_all(partial, "resp", 0, 0, axis_index_groups=SAME_CORE)
    upper_query = query_grads(upper_slopes, upper_prompt_keys, upper_span_keys)
    blocks, upper_query = lax.optimization_barrier((blocks, upper_query))
    part = project(
        head,
        blocks,
        (upper_key_weight, upper_value_weight, lower_key_weight, lower_value_weight),
        (own, near, *below, *above, *across),
    )
    part, lower_slopes = lax.optimization_barrier((part, lower_slopes))
    blocks = lax.all_to_all(part, "head", 0, 0)
    lower_query = query_grads(lower_slopes, lower_prompt_keys, lower_span_keys)
    prompt_grads = jnp.sum(blocks.astype(jnp.float32), axis=0).astype(jnp.bfloat16)
    return (upper_query, lower_query, upper_span, lower_span, prompt_grads)


def solution(mesh):
    layer = (
        P("resp", "head"), P("head"), P(None, "head"), P(None, "head"), P(None, "head"),
        P(None, "head"), P("resp", "head"), P("resp", "head"), P("resp", "head"), P("resp", "head"),
    )
    return jax.shard_map(
        body,
        mesh=mesh,
        in_specs=layer + layer,
        out_specs=(P("resp", "head"),) * 5,
        check_vma=False,
    )
```

```python
import functools
import jax
import jax.numpy as jnp
from jax import lax
from jax.experimental import pallas as pl
from jax.experimental.pallas import tpu as pltpu
from jax.sharding import PartitionSpec as P

HEAD = 128
C = 64
NT = (((1,), (1,)), ((), ()))
LAG = 6
TN = (((0,), (0,)), ((), ()))


def attend_kernel(core_ref, q_hbm, g_hbm, k_hbm, v_hbm, sk_hbm, sv_hbm, slopes_hbm, span_hbm,
                  mine_hbm, other_hbm, scores, dots, key_sums, value_sums,
                  q_ref, g_ref, k_ref, v_ref, sk_ref, sv_ref, sems,
                  slopes_ref, span_ref, mine_ref, other_ref, out_sems):
    copies = [
        pltpu.make_async_copy(source, target, sems.at[i])
        for i, (source, target) in enumerate((
            (q_hbm, q_ref), (k_hbm, k_ref), (sk_hbm, sk_ref), (g_hbm, g_ref), (v_hbm, v_ref),
            (sv_hbm, sv_ref),
        ))
    ]
    for copy in copies:
        copy.start()
    for copy in copies[:2]:
        copy.wait()
    tokens = q_ref.shape[0]
    prompt = k_ref.shape[0]
    group = 2
    pair = group * tokens
    pairs = q_ref.shape[1] // (group * HEAD)
    scale = HEAD ** -0.5
    factor = scale * 1.4426950408889634
    chunk = 2 * C
    count = prompt // chunk + 1
    parts = [slice(j * chunk, (j + 1) * chunk) for j in range(count)]
    even = core_ref[0] == 0

    def rows_of(ref, span, j):
        return ref[parts[j], :] if j < count - 1 else span[...]

    def stacked(ref, p):
        heads = [ref[:, h * HEAD:(h + 1) * HEAD] for h in range(group * p, group * p + group)]
        return jnp.concatenate(heads, axis=0)

    def first_pass(p, state):
        query = stacked(q_ref, p)
        grad = None if p == 0 else stacked(g_ref, p)
        tops = []
        totals = []
        deltas = []
        for j in range(count):
            block = lax.dot_general(
                rows_of(k_ref, sk_ref, j), query, NT, preferred_element_type=jnp.float32
            )
            if j == count - 1:
                u = lax.broadcasted_iota(jnp.int32, block.shape, 0)
                t = lax.rem(lax.broadcasted_iota(jnp.int32, block.shape, 1), tokens)
                block = jnp.where((lax.div(u, C) == lax.div(t, C)) & (u <= t), block, -1e30)
            top = jnp.max(block, axis=0, keepdims=True)
            block = jnp.exp2((block - top) * factor)
            scores[p, parts[j], :] = block
            if grad is None:
                for copy in copies[2:]:
                    copy.wait()
                grad = stacked(g_ref, p)
            dot = lax.dot_general(
                rows_of(v_ref, sv_ref, j), grad, NT, preferred_element_type=jnp.float32
            )
            dots[p, parts[j], :] = dot
            tops.append(top)
            totals.append(jnp.sum(block, axis=0, keepdims=True))
            deltas.append(jnp.sum(block * dot, axis=0, keepdims=True))
            yield
        tops = jnp.concatenate(tops, axis=0)
        weigh = jnp.exp2((tops - jnp.max(tops, axis=0, keepdims=True)) * factor)
        total = jnp.sum(weigh * jnp.concatenate(totals, axis=0), axis=0, keepdims=True)
        weigh = weigh / total
        delta = jnp.sum(weigh * jnp.concatenate(deltas, axis=0), axis=0, keepdims=True)
        state[p] = (query, grad, weigh, delta)

    def second_pass(p, state):
        query, grad, weigh, delta = state.pop(p)
        for j in range(count):
            weight = scores[p, parts[j], :] * weigh[j:j + 1, :]
            slope = (weight * (dots[p, parts[j], :] - delta)).astype(jnp.bfloat16)
            weight = weight.astype(jnp.bfloat16)
            slopes_ref[p, parts[j], :] = slope
            key_sum = jnp.dot(slope, query, preferred_element_type=jnp.float32)
            value_sum = jnp.dot(weight, grad, preferred_element_type=jnp.float32)
            if p > 0:
                key_sum = key_sum + key_sums[parts[j], :]
                value_sum = value_sum + value_sums[parts[j], :]
            if p < pairs - 1:
                key_sums[parts[j], :] = key_sum
                value_sums[parts[j], :] = value_sum
            else:
                both = jnp.concatenate([key_sum * scale, value_sum], axis=1)
                if j == count - 1:
                    span_ref[...] = both.astype(jnp.bfloat16)
                    send(span_ref, span_hbm)
                else:
                    half = slice(j * C, (j + 1) * C)
                    mine_ref[half, :] = jnp.where(even, both[:C], both[C:]).astype(jnp.bfloat16)
                    other_ref[half, :] = jnp.where(even, both[C:], both[:C]).astype(jnp.bfloat16)
                    if j % 4 == 3:
                        ready = slice((j - 3) * C, (j + 1) * C)
                        send(other_ref.at[ready, :], other_hbm.at[ready, :])
                        send(mine_ref.at[ready, :], mine_hbm.at[ready, :])
            yield
        send(slopes_ref.at[p], slopes_hbm.at[p])

    outs = []

    def send(source, target):
        copy = pltpu.make_async_copy(source, target, out_sems.at[len(outs)])
        copy.start()
        outs.append(copy)

    state = {}

    def chained(one):
        for p in range(pairs):
            yield from one(p, state)

    first = chained(first_pass)
    second = chained(second_pass)
    for ahead in range(count + LAG):
        next(first)
    for unused in second:
        next(first, None)
    for copy in outs:
        copy.wait()


def attend(core, q, k, v, sk, sv, g):
    tokens = q.shape[0]
    heads = q.shape[1] // HEAD
    prompt = k.shape[0]
    rows = prompt + tokens

    def whole(*shape):
        return pl.BlockSpec(shape, lambda i, core: (0, 0))

    paired = whole(tokens, heads * HEAD)
    return pl.pallas_call(
        attend_kernel,
        grid_spec=pltpu.PrefetchScalarGridSpec(
            num_scalar_prefetch=1,
            grid=(1,),
            in_specs=[
                pl.BlockSpec(memory_space=pl.ANY)
            ] * 6,
            out_specs=[pl.BlockSpec(memory_space=pl.ANY)] * 4,
            scratch_shapes=[
                pltpu.VMEM((heads // 2, rows, 2 * tokens), jnp.float32),
                pltpu.VMEM((heads // 2, rows, 2 * tokens), jnp.float32),
                pltpu.VMEM((rows, HEAD), jnp.float32),
                pltpu.VMEM((rows, HEAD), jnp.float32),
                pltpu.VMEM(q.shape, jnp.bfloat16),
                pltpu.VMEM(g.shape, jnp.bfloat16),
                pltpu.VMEM(k.shape, jnp.bfloat16),
                pltpu.VMEM(v.shape, jnp.bfloat16),
                pltpu.VMEM(sk.shape, jnp.bfloat16),
                pltpu.VMEM(sv.shape, jnp.bfloat16),
                pltpu.SemaphoreType.DMA((6,)),
                pltpu.VMEM((heads // 2, rows, 2 * tokens), jnp.bfloat16),
                pltpu.VMEM((tokens, 2 * HEAD), jnp.bfloat16),
                pltpu.VMEM((prompt // 2, 2 * HEAD), jnp.bfloat16),
                pltpu.VMEM((prompt // 2, 2 * HEAD), jnp.bfloat16),
                pltpu.SemaphoreType.DMA((13,)),
            ],
        ),
        out_shape=[
            jax.ShapeDtypeStruct((heads // 2, rows, 2 * tokens), jnp.bfloat16),
            jax.ShapeDtypeStruct((tokens, 2 * HEAD), jnp.bfloat16),
            jax.ShapeDtypeStruct((prompt // 2, 2 * HEAD), jnp.bfloat16),
            jax.ShapeDtypeStruct((prompt // 2, 2 * HEAD), jnp.bfloat16),
        ],
        compiler_params=pltpu.CompilerParams(vmem_limit_bytes=62 * 1024 * 1024),
        cost_estimate=pl.CostEstimate(
            flops=10 * rows * heads * tokens * HEAD,
            bytes_accessed=4 * 1024 * 1024,
            transcendentals=rows * heads * tokens,
        ),
    )(core, q, g, k, v, sk, sv)


def query_kernel(slopes_ref, k_ref, sk_ref, dq_ref):
    prompt = k_ref.shape[0]
    tokens = dq_ref.shape[0]
    sums = lax.dot_general(
        slopes_ref[0, :prompt, :], k_ref[...], TN, preferred_element_type=jnp.float32
    ) + lax.dot_general(
        slopes_ref[0, prompt:, :], sk_ref[...], TN, preferred_element_type=jnp.float32
    )
    sums = (sums * HEAD ** -0.5).astype(jnp.bfloat16)
    dq_ref[:, :HEAD] = sums[:tokens]
    dq_ref[:, HEAD:] = sums[tokens:]


def query_grads(slopes, k, sk):
    pairs, rows, width = slopes.shape
    tokens = sk.shape[0]
    return pl.pallas_call(
        query_kernel,
        grid=(pairs,),
        in_specs=[
            pl.BlockSpec((1, rows, width), lambda i: (i, 0, 0)),
            pl.BlockSpec(k.shape, lambda i: (0, 0)),
            pl.BlockSpec(sk.shape, lambda i: (0, 0)),
        ],
        out_specs=pl.BlockSpec((tokens, width), lambda i: (0, i)),
        out_shape=jax.ShapeDtypeStruct((tokens, pairs * width), jnp.bfloat16),
        compiler_params=pltpu.CompilerParams(vmem_limit_bytes=62 * 1024 * 1024),
        cost_estimate=pl.CostEstimate(
            flops=2 * pairs * rows * width * HEAD,
            bytes_accessed=6 * 1024 * 1024,
            transcendentals=0,
        ),
    )(slopes, k, sk)


D = 5120
epsilon = 1e-06
RESP = 32
HEADS = 8
CORE_SWAP = [(i, i ^ 1) for i in range(RESP)]
FAR_SWAP = [(i, i ^ 16) for i in range(RESP)]
SAME_CORE = [[2 * i + c for i in range(RESP // 2)] for c in range(2)]
NEAR_SWAP = [(i, i ^ 4) for i in range(HEADS)]
UP = [(i, i // 4 * 4 + (i + 1) % 4) for i in range(HEADS)]
DOWN = [(i, i // 4 * 4 + (i + 3) % 4) for i in range(HEADS)]
ACROSS = [(i, i ^ 2) for i in range(HEADS)]
EXTRA = 16
SMEM = pl.BlockSpec(memory_space=pltpu.SMEM)
BIG_VMEM = pltpu.CompilerParams(vmem_limit_bytes=62 * 1024 * 1024)


def cost(read, flops=0):
    return pl.CostEstimate(flops=flops, bytes_accessed=read, transcendentals=0)


def pack_kernel(upper_ref, lower_ref, upper_gain_ref, lower_gain_ref, out_ref):
    rows, width = upper_ref.shape
    place = lax.broadcasted_iota(jnp.int32, (EXTRA, width), 0)
    upper_gain = upper_gain_ref[...].astype(jnp.float32).reshape(1, width)
    lower_gain = lower_gain_ref[...].astype(jnp.float32).reshape(1, width)
    gains = jnp.where(place == 0, upper_gain, jnp.where(place == 1, lower_gain, 0.0))
    out_ref[:rows, :] = upper_ref[...]
    out_ref[rows : 2 * rows, :] = lower_ref[...]
    out_ref[2 * rows :, :] = gains.astype(jnp.bfloat16)


def pack(upper_input, lower_input, upper_gain, lower_gain):
    rows, width = upper_input.shape
    return pl.pallas_call(
        pack_kernel,
        out_shape=jax.ShapeDtypeStruct((2 * rows + EXTRA, width), jnp.bfloat16),
        compiler_params=BIG_VMEM,
        cost_estimate=cost(400000),
    )(upper_input, lower_input, upper_gain, lower_gain)


def split(far, mine, got):
    total = mine.astype(jnp.float32) + got.astype(jnp.float32)
    total = total.astype(jnp.bfloat16).reshape(RESP // 2, 2, -1, mine.shape[1])
    low = far == 0
    kept = jnp.where(low, total[:, 0], total[:, 1])
    sent = jnp.where(low, total[:, 1], total[:, 0])
    return kept, sent


def join(kept, far, mine, got):
    upper = (kept.astype(jnp.float32) + far.astype(jnp.float32)).astype(jnp.bfloat16)
    lower = (mine.astype(jnp.float32) + got.astype(jnp.float32)).astype(jnp.bfloat16)
    return jnp.concatenate([upper, lower.reshape(RESP // 2, -1, mine.shape[1])], axis=1)


def project_kernel(head_ref, blocks_hbm, *refs):
    piece_hbm = refs[:8]
    weight_hbm = refs[8:12]
    out_ref, blocks_ref, pieces_ref, weights_ref, scaled, sems, piece_sems = refs[12:]
    piece_refs = [pieces_ref.at[i] for i in range(8)]
    count, rows, width = out_ref.shape
    half = rows // 2
    sources = blocks_ref.shape[0]
    copies = [
        pltpu.make_async_copy(
            source, weights_ref.at[w // 2, :, pl.ds(w % 2 * HEAD, HEAD)], sems.at[w]
        )
        for w, source in enumerate(weight_hbm)
    ]
    blocks_copy = pltpu.make_async_copy(blocks_hbm, blocks_ref, piece_sems.at[8])
    piece_copies = [
        pltpu.make_async_copy(source, target, piece_sems.at[i])
        for i, (source, target) in enumerate(zip(piece_hbm, piece_refs))
    ]
    for copy in [blocks_copy] + copies[:2] + piece_copies + copies[2:]:
        copy.start()
    blocks_copy.wait()

    def total(first, last, part):
        summed = blocks_ref[first, part, :].astype(jnp.float32)
        for i in range(first + 1, last):
            summed = summed + blocks_ref[i, part, :].astype(jnp.float32)
        return summed.astype(jnp.bfloat16)

    upper = jnp.concatenate(
        [
            total(0, sources // 2, slice(0, half)),
            total(sources // 2, sources, slice(0, half)),
        ],
        axis=0,
    )
    lower = total(0, sources, slice(half, 3 * half))
    near = lax.div(head_ref[0], 4)
    across = lax.rem(head_ref[0], 4)
    owners = []
    for shift in (0, 3, 1, 2):
        for side in (near, 1 - near):
            owners.append(side * 4 + lax.rem(across + shift, 4))
    inverses = []
    shrinks = []
    groups = width // 128
    for copy in piece_copies:
        copy.wait()

    def folded(values):
        return sum(values[:, g * 128 : (g + 1) * 128] for g in range(groups))

    for layer, rounded in enumerate((upper, lower)):
        place = slice(layer * rows, (layer + 1) * rows)
        squares = jnp.zeros((rows, 128), jnp.float32)
        sums = jnp.zeros((rows, 128), jnp.float32)
        for piece_ref in piece_refs:
            hidden = piece_ref[place, :].astype(jnp.float32)
            squares = squares + folded(hidden * hidden)
        for copy in copies[2 * layer : 2 * layer + 2]:
            copy.wait()
        for i, (piece_ref, owner) in enumerate(zip(piece_refs, owners)):
            columns = pl.ds(pl.multiple_of(owner * width, 128), width)
            gains = piece_ref[2 * rows :, :].astype(jnp.float32)
            projected = lax.dot_general(
                rounded, weights_ref[layer, columns, :], NT, preferred_element_type=jnp.float32
            )
            one = projected * gains[layer : layer + 1]
            scaled[layer, i] = one
            sums = sums + folded(one * piece_ref[place, :].astype(jnp.float32))
        squares = jnp.sum(squares, axis=1, keepdims=True)
        sums = jnp.sum(sums, axis=1, keepdims=True)
        inverse = lax.rsqrt(squares / D + epsilon)
        inverses.append(inverse)
        shrinks.append(inverse * inverse * inverse * sums / D)
    for i, (piece_ref, owner) in enumerate(zip(piece_refs, owners)):
        part = jnp.zeros((rows, width), jnp.float32)
        for layer in range(2):
            hidden = piece_ref[layer * rows : (layer + 1) * rows, :].astype(jnp.float32)
            part = part + inverses[layer] * scaled[layer, i] - shrinks[layer] * hidden
        out_ref[owner] = part.astype(jnp.bfloat16)


def project(head, blocks, weights, pieces):
    rows = blocks.shape[1] // 3 * 2
    width = pieces[0].shape[1]
    vmem = pl.BlockSpec(memory_space=pltpu.VMEM)
    return pl.pallas_call(
        project_kernel,
        in_specs=[SMEM] + [pl.BlockSpec(memory_space=pl.ANY)] * 13,
        out_specs=vmem,
        out_shape=jax.ShapeDtypeStruct((HEADS, rows, width), jnp.bfloat16),
        scratch_shapes=[
            pltpu.VMEM(blocks.shape, jnp.bfloat16),
            pltpu.VMEM((HEADS,) + pieces[0].shape, jnp.bfloat16),
            pltpu.VMEM((2, D, 2 * HEAD), jnp.bfloat16),
            pltpu.VMEM((2, HEADS, rows, width), jnp.float32),
            pltpu.SemaphoreType.DMA((4,)),
            pltpu.SemaphoreType.DMA((9,)),
        ],
        compiler_params=pltpu.CompilerParams(vmem_limit_bytes=55 * 1024 * 1024),
        cost_estimate=cost(8000000, 8 * rows * D * HEAD),
    )(head, blocks, *pieces, *weights)


def body(
    upper_input, upper_gain, upper_key_weight, upper_value_weight, upper_prompt_keys,
    upper_prompt_values, upper_queries, upper_span_keys, upper_span_values, upper_out_grad,
    lower_input, lower_gain, lower_key_weight, lower_value_weight, lower_prompt_keys,
    lower_prompt_values, lower_queries, lower_span_keys, lower_span_values, lower_out_grad,
):
    place = lax.axis_index("resp").astype(jnp.int32)
    core = lax.rem(place, 2).reshape(1)
    far = lax.div(place, 16)
    head = lax.axis_index("head").astype(jnp.int32).reshape(1)
    upper_slopes, upper_span, mine, other = attend(
        core, upper_queries, upper_prompt_keys, upper_prompt_values, upper_span_keys,
        upper_span_values, upper_out_grad,
    )
    other, upper_input = lax.optimization_barrier((other, upper_input))
    got = lax.ppermute(other, "resp", CORE_SWAP)
    own = pack(upper_input, lower_input, upper_gain, lower_gain)
    kept, sent = split(far, mine, got)
    sent, own, lower_queries = lax.optimization_barrier((sent, own, lower_queries))
    from_far = lax.ppermute(sent, "resp", FAR_SWAP)
    near = lax.ppermute(own, "head", NEAR_SWAP)
    lower_slopes, lower_span, mine, other = attend(
        core, lower_queries, lower_prompt_keys, lower_prompt_values, lower_span_keys,
        lower_span_values, lower_out_grad,
    )
    other, from_far, near = lax.optimization_barrier((other, from_far, near))
    got = lax.ppermute(other, "resp", CORE_SWAP)
    partial = join(kept, from_far, mine, got)
    partial, own, near, upper_slopes = lax.optimization_barrier((partial, own, near, upper_slopes))
    below = [lax.ppermute(one, "head", UP) for one in (own, near)]
    across = [lax.ppermute(one, "head", ACROSS) for one in (own, near)]
    above = [lax.ppermute(one, "head", DOWN) for one in (own, near)]
    blocks = lax.all_to_all(partial, "resp", 0, 0, axis_index_groups=SAME_CORE)
    upper_query = query_grads(upper_slopes, upper_prompt_keys, upper_span_keys)
    blocks, upper_query = lax.optimization_barrier((blocks, upper_query))
    part = project(
        head,
        blocks,
        (upper_key_weight, upper_value_weight, lower_key_weight, lower_value_weight),
        (own, near, *below, *above, *across),
    )
    part, lower_slopes = lax.optimization_barrier((part, lower_slopes))
    blocks = lax.all_to_all(part, "head", 0, 0)
    lower_query = query_grads(lower_slopes, lower_prompt_keys, lower_span_keys)
    prompt_grads = jnp.sum(blocks.astype(jnp.float32), axis=0).astype(jnp.bfloat16)
    return (upper_query, lower_query, upper_span, lower_span, prompt_grads)


def solution(mesh):
    layer = (
        P("resp", "head"), P("head"), P(None, "head"), P(None, "head"), P(None, "head"),
        P(None, "head"), P("resp", "head"), P("resp", "head"), P("resp", "head"), P("resp", "head"),
    )
    return jax.shard_map(
        body,
        mesh=mesh,
        in_specs=layer + layer,
        out_specs=(P("resp", "head"),) * 5,
        check_vma=False,
    )
```
